32 devices in a mesh: tm: 8 (over z, y), eval: 4 (over x, core).
Axes of the slice: x: 2, y: 2, z: 4, core: 2. Of those that a mesh axis runs over, the one named last changes fastest.
Arguments:
- hidden: bfloat16 [128, 1024, 1536], P('tm', 'eval'), may hold values from -9 to 9
- modulation: float32 [128, 2, 1536], P('tm'), may hold values from -2 to 3
- head_weight: bfloat16 [64, 1536], replicated, may hold values from -1 to 1
- real_score: bfloat16 [32, 21, 16, 4096], P('eval', None, None, 'tm'), may hold values from -152917 to 152917
- fake_score: bfloat16 [32, 21, 16, 4096], P('eval', None, None, 'tm'), may hold values from -152917 to 152917
- window_start: int32 [32], P('eval'), may hold values from 0 to 107, as said below
- timestep: int32 [32], P('eval'), may hold values from 20 to 999
Outputs:
- d_hidden: bfloat16 [128, 1024, 1536], P('tm', 'eval')
- head_grad: float32 [64, 1536], replicated
- mod_grad: float32 [128, 2, 1536], P('tm')
The draws below stay inside these ranges and needn't reach their ends.
Inputs may be any that keep to these rules, and one draw needn't show every extreme that they name: `window_start`: every window lies inside the rollout; one window starts at frame 0 and one at the last possible frame.
All inputs are finite; a program needn't handle non-finite values.
Results may differ from the reference program's by a relative error of at most 0.0012.
The reference program's roundings to bfloat16 on the way (of `adapted`, `latent` and `upstream`) count: a program that leaves them out, or rounds other values in their place, can miss the bound.
Values may be sent and summed in bfloat16 or wider, within the bound.
A program may use at most 128 MiB of HBM per device.

```python
import math
import jax
import jax.numpy as jnp
from jax import lax

D = 1536
C = 16
PATCH = 4
WIN = 21
FD = 16
TOK = 1024
NW_DEV = 8
NWIN = 32
N_TM = 8
N_EVAL = 4


spike_count = 24


def spike_field(key):
    count = NW_DEV * N_EVAL
    entries = WIN * C * TOK * PATCH
    stratum = entries // spike_count
    offsets = jax.random.randint(jax.random.fold_in(key, 41), (count, spike_count), 0, stratum)
    spots = (jnp.arange(spike_count, dtype=jnp.int32)[None, :] * stratum + offsets).astype(jnp.int32)
    signs = (jax.random.randint(jax.random.fold_in(key, 42), (count, spike_count), 0, 2) * 2 - 1).astype(jnp.float32)
    levels = jnp.exp(jax.random.uniform(jax.random.fold_in(key, 43), (count, spike_count), jnp.float32, 0.0, math.log(10.0))) * (math.log(10.0) / 9.0)
    amounts = signs * levels * (0.04 * entries)
    return (spots, amounts)


def place_spikes(key, base):
    count = NW_DEV * N_EVAL
    spots, amounts = spike_field(key)
    window_rows = jnp.arange(count, dtype=jnp.int32)[:, None]
    flat = base.reshape(count, WIN * C * TOK * PATCH).at[window_rows, spots].set(amounts)
    return flat.reshape(base.shape).astype(jnp.bfloat16)


def shared_direction(key):
    bits = jax.random.randint(jax.random.fold_in(key, 51), (D,), 0, 2)
    return (bits * 2 - 1).astype(jnp.float32)


def draw_hidden(key, part):
    shape = (FD * N_TM, TOK, D)
    direction = shared_direction(key)
    noise = jnp.clip(jax.random.normal(jax.random.fold_in(key, 53), shape, jnp.float32), -6.0, 6.0)
    strength = 3.0 * jnp.arange(TOK, dtype=jnp.float32) / TOK
    values = noise + strength[None, :, None] * direction[None, None, :]
    return values.astype(jnp.bfloat16)


def draw_head_weight(key, part):
    direction = shared_direction(key)
    base = jnp.clip(jax.random.normal(jax.random.fold_in(key, 54), (C * PATCH, D), jnp.float32), -6.0, 6.0)
    loads = jnp.clip(jax.random.normal(jax.random.fold_in(key, 55), (C * PATCH,), jnp.float32), -3.0, 3.0)
    values = base / math.sqrt(D) + 2.0 * loads[:, None] * direction[None, :] / D
    return values.astype(jnp.bfloat16)


def draw_modulation(key, part):
    frames = FD * N_TM
    levels = jnp.exp(jax.random.uniform(jax.random.fold_in(key, 61), (frames, 1), jnp.float32, math.log(0.3), math.log(3.0)))
    scale_noise = 0.3 * jnp.clip(jax.random.normal(jax.random.fold_in(key, 64), (frames, D), jnp.float32), -3.0, 3.0)
    shift = 0.5 * jnp.clip(jax.random.normal(jax.random.fold_in(key, 65), (frames, D), jnp.float32), -3.0, 3.0)
    scale = levels - 1.0 + scale_noise
    return jnp.stack([shift, scale], axis=1).astype(jnp.float32)


def draw_real_score(key, part):
    shape = (NW_DEV * N_EVAL, WIN, C, TOK * PATCH)
    ramp = 1.0 + 2.0 * jnp.arange(TOK * PATCH, dtype=jnp.float32) / (TOK * PATCH)
    values = jnp.clip(jax.random.normal(jax.random.fold_in(key, 13), shape, jnp.float32), -6.0, 6.0)
    base = values * ramp
    return place_spikes(key, base)


def draw_fake_score(key, part):
    shape = (NW_DEV * N_EVAL, WIN, C, TOK * PATCH)
    base = jnp.clip(jax.random.normal(jax.random.fold_in(key, 15), shape, jnp.float32), -6.0, 6.0)
    return place_spikes(key, base)


def draw_window_start(key, part):
    count = NW_DEV * N_EVAL
    limit = FD * N_TM - WIN
    starts = jax.random.randint(jax.random.fold_in(key, 21), (count,), 0, limit + 1)
    starts = starts.at[0].set(0)
    starts = starts.at[count - 1].set(limit)
    return starts.astype(jnp.int32)


def with_ends(result, own_key, smallest, high):
    longest = result.shape.index(max(result.shape))
    spots = []
    for shift in (0, 1):
        where = [jax.random.randint(jax.random.fold_in(own_key, axis), (), 0, length) for axis, length in enumerate(result.shape)]
        where[longest] = (where[longest] + shift) % result.shape[longest]
        spots.append(tuple(where))
    return result.at[spots[0]].set(smallest).at[spots[1]].set(high)


def setup_inputs(seed: int = 0) -> dict:
    splits = jax.random.split(jax.random.key(seed), 8)
    hidden = draw_hidden(jax.random.fold_in(splits[7], 71), 0)
    modulation = draw_modulation(jax.random.fold_in(splits[7], 71), 0)
    head_weight = draw_head_weight(jax.random.fold_in(splits[7], 71), 0)
    real_score = draw_real_score(jax.random.fold_in(splits[7], 71), 0)
    fake_score = draw_fake_score(jax.random.fold_in(splits[7], 71), 0)
    window_start = draw_window_start(jax.random.fold_in(splits[7], 71), 0)
    timestep = with_ends(jax.random.randint(splits[6], (NWIN,), 20, 1000), jax.random.fold_in(splits[6], 1), 20, 999).astype(jnp.int32)
    return dict(hidden=hidden, modulation=modulation, head_weight=head_weight, real_score=real_score, fake_score=fake_score, window_start=window_start, timestep=timestep)


def layer_norm(frame):
    values = frame.astype(jnp.float32)
    center = lax.optimization_barrier(jnp.mean(values, axis=-1, keepdims=True))
    shifted = values - center
    inv_std = lax.rsqrt(lax.optimization_barrier(jnp.mean(shifted * shifted, axis=-1, keepdims=True)) + 1e-06)
    return (shifted * inv_std, inv_std)

def reference(hidden, modulation, head_weight, real_score, fake_score, window_start, timestep):

    def forward(pair):
        frame, shift_scale = pair
        normed, inv_std = layer_norm(frame)
        adapted = (normed * (1.0 + shift_scale[1]) + shift_scale[0]).astype(jnp.bfloat16)
        output = jnp.dot(adapted, head_weight.T, preferred_element_type=jnp.float32)
        return output.astype(jnp.bfloat16).reshape(TOK, C, PATCH).transpose(1, 0, 2).reshape(C, TOK * PATCH)
    latent = lax.map(forward, (hidden, modulation))

    def add_window(total, items):
        start, level, real, fake = items
        start = start.astype(jnp.int32)
        block = lax.dynamic_slice_in_dim(latent, start, WIN, 0).astype(jnp.float32)
        real_values = real.astype(jnp.float32)
        fake_values = fake.astype(jnp.float32)
        normalizer = jnp.sum(jnp.abs(block - real_values)) / (WIN * C * PATCH * TOK) + 1e-05
        weight = level.astype(jnp.float32) / 1000.0 / normalizer
        window_grad = weight * (fake_values - real_values)
        current = lax.dynamic_slice_in_dim(total, start, WIN, 0)
        return (lax.dynamic_update_slice_in_dim(total, current + window_grad, start, 0), None)
    empty = jnp.zeros((FD * N_TM, C, TOK * PATCH), jnp.float32)
    frame_grad, _ = lax.scan(add_window, empty, (window_start, timestep, real_score, fake_score))

    def backward(total, items):
        frame, shift_scale, grad = items
        normed, inv_std = layer_norm(frame)
        adapted = (normed * (1.0 + shift_scale[1]) + shift_scale[0]).astype(jnp.bfloat16)
        upstream = grad.reshape(C, TOK, PATCH).transpose(1, 0, 2).reshape(TOK, C * PATCH).astype(jnp.bfloat16)
        d_adapted = jnp.dot(upstream, head_weight, preferred_element_type=jnp.float32)
        head_part = jnp.dot(upstream.T, adapted, preferred_element_type=jnp.float32)
        mod_part = jnp.stack([lax.optimization_barrier(jnp.sum(d_adapted, axis=0)), lax.optimization_barrier(jnp.sum(d_adapted * normed, axis=0))])
        d_normed = d_adapted * (1.0 + shift_scale[1])
        d_hidden = inv_std * (d_normed - lax.optimization_barrier(jnp.mean(d_normed, axis=-1, keepdims=True)) - normed * lax.optimization_barrier(jnp.mean(d_normed * normed, axis=-1, keepdims=True)))
        return (total + head_part, (d_hidden.astype(jnp.bfloat16), mod_part))
    start_head = jnp.zeros((C * PATCH, hidden.shape[2]), jnp.float32)
    head_grad, (d_hidden, mod_grad) = lax.scan(backward, start_head, (hidden, modulation, frame_grad))
    return (d_hidden, head_grad, mod_grad)
```

```python
import functools

import jax
import jax.numpy as jnp
from jax import lax
from jax.experimental import pallas as pl
from jax.experimental.pallas import tpu as pltpu
from jax.sharding import PartitionSpec as P

C = 16
PATCH = 4
WIN = 21
TOK = 1024
EPS = 1e-06
LANES = 128
ROWS = 16
MESH = pl.DeviceIdType.MESH
VMEM_LIMIT = 56 * 1024 * 1024
F32 = jnp.float32
BF16 = jnp.bfloat16


def remote(src, dst, send_sem, recv_sem, device):
    return pltpu.make_async_remote_copy(
        src_ref=src, dst_ref=dst, send_sem=send_sem, recv_sem=recv_sem, device_id=device, device_id_type=MESH
    )


def greet(device):
    pl.semaphore_signal(pltpu.get_barrier_semaphore(), inc=1, device_id=device, device_id_type=MESH)


def when_not(flag, action):
    pl.when(jnp.logical_not(flag))(action)


def pixel_permutation(inverse):
    size = PATCH * LANES
    lane = lax.broadcasted_iota(jnp.int32, (size, size), 1 if inverse else 0)
    pixel = lax.broadcasted_iota(jnp.int32, (size, size), 0 if inverse else 1)
    return jnp.where(pixel == (lane & (LANES - 1)) * PATCH + (lane >> 7), 1.0, 0.0).astype(BF16)


def row_permutation(inverse):
    size = C * PATCH
    grouped = lax.broadcasted_iota(jnp.int32, (size, size), 1 if inverse else 0)
    mixed = lax.broadcasted_iota(jnp.int32, (size, size), 0 if inverse else 1)
    return jnp.where(mixed == (grouped & (C - 1)) * PATCH + (grouped >> 4), 1.0, 0.0).astype(BF16)


def dot(a, b, dims=((1,), (0,))):
    return lax.dot_general(a, b, (dims, ((), ())), preferred_element_type=F32)


def forward_kernel(
    n_tm, n_eval, n_blk, starts, hidden, modulation, weight, real, totals, stats,
    adapted, perm, rows, mine, latent, sums, out_send, out_recv, x_send, x_recv, c_send, c_recv, s_send, s_recv,
):
    frame = pl.program_id(0)
    frames = pl.num_programs(0)
    fd = mine.shape[0]
    last = fd - 1
    t = lax.axis_index("tm")
    e = lax.axis_index("eval")
    n_x = n_eval // 2
    x, core = e // 2, e % 2
    partner = 2 * x + 1 - core
    per = fd // n_eval
    tok, width = hidden.shape[1], hidden.shape[2]
    n_win = real.shape[0]

    @pl.when(frame == 0)
    def _():
        source = t // n_blk
        for other in range(n_tm):
            when_not((other == t) & (source == e), lambda: greet((other, source)))
            when_not(other == t, lambda: greet((other, e)))
        for other in range(n_eval):
            when_not(other == e, lambda: greet((t, other)))
        own = jnp.where(source == e, 1, 0)
        pl.semaphore_wait(pltpu.get_barrier_semaphore(), n_tm - own + n_tm - 1 + n_eval - 1)
        perm[...] = pixel_permutation(False)
        rows[...] = row_permutation(False)

    shift = modulation[0, 0:1, :]
    scale = 1.0 + modulation[0, 1:2, :]
    lane = lax.broadcasted_iota(jnp.int32, (ROWS, LANES), 1)

    def chunk(i, carry):
        at = pl.ds(pl.multiple_of(i * ROWS, ROWS), ROWS)
        values = hidden[0, at, :].astype(F32)
        center = jnp.sum(values, axis=1, keepdims=True) * (1.0 / width)
        shifted = values - center
        inv_std = lax.rsqrt(jnp.sum(shifted * shifted, axis=1, keepdims=True) * (1.0 / width) + EPS)
        adapted[at, :] = (shifted * inv_std * scale + shift).astype(BF16)
        stats[0, at, :] = jnp.where(lane == 0, center, inv_std)
        return carry

    lax.fori_loop(0, tok // ROWS, chunk, 0, unroll=2)
    out = dot(weight[...], adapted[...], ((1,), (1,))).astype(BF16)
    grouped = dot(rows[...], out).astype(BF16)
    pixels = []
    for j in range(tok // LANES):
        tile = grouped[:, j * LANES : (j + 1) * LANES]
        wide = jnp.concatenate([tile[s * C : (s + 1) * C] for s in range(PATCH)], axis=1)
        pixels.append(dot(wide, perm[...]).astype(BF16))
    pixels = jnp.concatenate(pixels, axis=1)
    pixel_block = mine.shape[3]
    target = frame % n_eval
    place = frame // n_eval
    for b in range(n_blk):
        mine[frame, b] = pixels[:, b * pixel_block : (b + 1) * pixel_block]
    for b in range(n_blk):
        owner = e * n_blk + b
        own = (owner == t) & (target == e)
        dst = latent.at[target, place, t]

        @pl.when(own)
        def _():
            pltpu.make_async_copy(mine.at[frame, b], dst, out_recv.at[place, t]).start()

        @pl.when(jnp.logical_not(own))
        def _():
            remote(mine.at[frame, b], dst, out_send.at[frame, b], out_recv.at[place, t], (owner, target)).start()

    def x_copy(r, d):
        there = 2 * ((x + d) % n_x) + core
        return remote(latent.at[e, r], latent.at[e, r], x_send.at[r, d - 1], x_recv.at[r, d - 1], (t, there))

    def core_copy(r, d):
        held = 2 * ((x + n_x - d) % n_x) + core
        return remote(latent.at[held, r], latent.at[held, r], c_send.at[r, d], c_recv.at[r, d], (t, partner))

    def first(r):
        for source in range(n_tm):
            pltpu.make_async_copy(mine.at[0, 0], latent.at[e, r, source], out_recv.at[r, source]).wait()
        for d in range(1, n_x):
            x_copy(r, d).start()
        core_copy(r, 0).start()

    def second(r):
        for d in range(1, n_x):
            x_copy(r, d).wait_recv()
            core_copy(r, d).start()

    for r in range(per):
        pl.when(frame == min((r + 2) * n_eval - 1, last))(functools.partial(first, r))
    for r in range(per):
        pl.when(frame == min((r + 3) * n_eval - 1, last))(functools.partial(second, r))

    @pl.when(frame == frames - 1)
    def _():
        for f in range(fd):
            for b in range(n_blk):
                owner = e * n_blk + b
                own = (owner == t) & (f % n_eval == e)
                when_not(
                    own,
                    lambda: remote(
                        mine.at[f, b], mine.at[f, b], out_send.at[f, b], out_recv.at[0, 0], (owner, f % n_eval)
                    ).wait_send(),
                )
        for r in range(per):
            for d in range(1, n_x):
                x_copy(r, d).wait_send()
            for d in range(n_x):
                core_copy(r, d).wait()
        row = lax.broadcasted_iota(jnp.int32, (n_win, LANES), 0)
        found = jnp.zeros((n_win, LANES), F32)
        for w in range(n_win):
            start = starts[w]

            def add(k, acc):
                g = start + k
                inner = g % fd
                block = latent[inner % n_eval, inner // n_eval, g // fd].astype(F32)
                return acc + jnp.abs(block - real[w, k].astype(F32))

            acc = lax.fori_loop(0, WIN, add, jnp.zeros(real.shape[2:], F32), unroll=3)
            total = jnp.sum(jnp.sum(acc, axis=0, keepdims=True), axis=1, keepdims=True)
            found = jnp.where(row == w, total, found)
        sums[t] = found
        for d in range(1, n_tm):
            there = (t + d) % n_tm
            remote(sums.at[t], sums.at[t], s_send.at[d - 1], s_recv.at[d - 1], (there, e)).start()
        for d in range(1, n_tm):
            origin = (t + n_tm - d) % n_tm
            remote(sums.at[origin], sums.at[origin], s_send.at[d - 1], s_recv.at[d - 1], (origin, e)).wait()
        result = sums[0]
        for other in range(1, n_tm):
            result = result + sums[other]
        totals[...] = result


def window_kernel(n_pixels, starts, totals, times, real, fake, out):
    out[...] = jnp.zeros_like(out)
    level = times[...].astype(F32) / 1000.0 / (totals[...] / n_pixels + 1e-05)
    for w in range(real.shape[0]):
        start = starts[w]
        gain = level[w : w + 1, 0:1]

        def add(k, carry):
            out[start + k] += gain * (fake[w, k].astype(F32) - real[w, k].astype(F32))
            return carry

        lax.fori_loop(0, WIN, add, 0, unroll=3)


def reduce_kernel(
    n_tm, n_eval, n_blk, grad, out,
    from_core, half, from_x, rounded, landed, c_send, c_recv, x_send, x_recv, o_send, o_recv,
):
    t = lax.axis_index("tm")
    e = lax.axis_index("eval")
    n_x = n_eval // 2
    x, core = e // 2, e % 2
    partner = 2 * x + 1 - core
    fd = grad.shape[1]
    per = fd // n_eval
    mid = fd // 2
    home = t // n_blk
    slot = t % n_blk
    quarter = core * n_x + x

    for other in range(n_eval):
        when_not(other == e, lambda: greet((t, other)))
        for b in range(n_blk):
            when_not((e * n_blk + b == t) & (other == e), lambda: greet((e * n_blk + b, other)))
    own_home = jnp.where(home == e, 1, 0)
    pl.semaphore_wait(pltpu.get_barrier_semaphore(), n_eval - 1 + n_tm - own_home)

    def core_copy(o):
        return remote(
            grad.at[o, pl.ds((1 - core) * mid, mid)], from_core.at[o], c_send.at[o], c_recv.at[o], (t, partner)
        )

    def x_copy(o, d):
        there = (x + d) % n_x
        return remote(
            half.at[o, pl.ds(there * per, per)], from_x.at[o, d - 1], x_send.at[o, d - 1], x_recv.at[o, d - 1],
            (t, 2 * there + core),
        )

    def out_copy(o):
        return remote(
            rounded.at[o], landed.at[slot, quarter], o_send.at[o], o_recv.at[slot, quarter], (o, home)
        )

    def order(i):
        return (t + i) % n_tm

    def start_core(i, carry):
        core_copy(order(i)).start()
        return carry

    def combine(i, carry):
        o = order(i)
        core_copy(o).wait_recv()
        half[o] = grad[o, pl.ds(core * mid, mid)] + from_core[o]
        for d in range(1, n_x):
            x_copy(o, d).start()
        return carry

    def finish(i, carry):
        o = order(i)
        total = half[o, pl.ds(x * per, per)]
        for d in range(1, n_x):
            x_copy(o, d).wait_recv()
            total = total + from_x[o, d - 1]
        rounded[o] = total.astype(BF16)
        own = (o == t) & (home == e)

        @pl.when(own)
        def _():
            pltpu.make_async_copy(rounded.at[o], landed.at[slot, quarter], o_recv.at[slot, quarter]).start()

        @pl.when(jnp.logical_not(own))
        def _():
            out_copy(o).start()

        return carry

    def drain(i, carry):
        o = order(i)
        core_copy(o).wait_send()
        for d in range(1, n_x):
            x_copy(o, d).wait_send()
        when_not((o == t) & (home == e), lambda: out_copy(o).wait_send())
        return carry

    lax.fori_loop(0, n_tm, start_core, 0)
    lax.fori_loop(0, n_tm, combine, 0)
    lax.fori_loop(0, n_tm, finish, 0)
    lax.fori_loop(0, n_tm, drain, 0)
    for b in range(n_blk):
        for q in range(n_eval):
            pltpu.make_async_copy(rounded.at[0], landed.at[b, q], o_recv.at[b, q]).wait()
    pixel_block = grad.shape[3]
    for b in range(n_blk):
        out[:, :, b * pixel_block : (b + 1) * pixel_block] = landed[b].reshape(fd, C, pixel_block)


def backward_kernel(
    hidden, modulation, weight, stats, upstream, d_hidden, head_part, mod_part,
    adapted, d_adapted, perm, rows, sum_a, sum_b,
):
    frame = pl.program_id(0)
    tok, width = hidden.shape[1], hidden.shape[2]

    @pl.when(frame == 0)
    def _():
        perm[...] = pixel_permutation(True)
        rows[...] = row_permutation(True)
        head_part[...] = jnp.zeros_like(head_part)

    shift = modulation[0, 0:1, :]
    scale = 1.0 + modulation[0, 1:2, :]
    size = LANES * PATCH
    tiles = []
    for j in range(tok // LANES):
        wide = dot(upstream[0, :, j * size : (j + 1) * size], perm[...]).astype(BF16)
        tiles.append(jnp.concatenate([wide[:, s * LANES : (s + 1) * LANES] for s in range(PATCH)], axis=0))
    up = dot(rows[...], jnp.concatenate(tiles, axis=1)).astype(BF16)
    d_adapted[...] = dot(up, weight[...], ((0,), (0,)))
    sum_a[...] = jnp.zeros_like(sum_a)
    sum_b[...] = jnp.zeros_like(sum_b)

    def chunk(i, carry):
        at = pl.ds(pl.multiple_of(i * ROWS, ROWS), ROWS)
        center = stats[0, at, 0:1]
        inv_std = stats[0, at, 1:2]
        normed = (hidden[0, at, :].astype(F32) - center) * inv_std
        adapted[at, :] = (normed * scale + shift).astype(BF16)
        da = d_adapted[at, :]
        cross = da * normed
        sum_a[...] += da[0:8] + da[8:16]
        sum_b[...] += cross[0:8] + cross[8:16]
        dn = da * scale
        mean_a = jnp.sum(dn, axis=1, keepdims=True) * (1.0 / width)
        mean_b = jnp.sum(cross * scale, axis=1, keepdims=True) * (1.0 / width)
        d_hidden[0, at, :] = (inv_std * (dn - mean_a - normed * mean_b)).astype(BF16)
        return carry

    lax.fori_loop(0, tok // ROWS, chunk, 0, unroll=2)
    head_part[...] += dot(up, adapted[...])
    mod_part[0, 0:1, :] = jnp.sum(sum_a[...], axis=0, keepdims=True)
    mod_part[0, 1:2, :] = jnp.sum(sum_b[...], axis=0, keepdims=True)


def sum_kernel(
    n_tm, n_eval, head, mod, head_out, mod_out,
    from_eval, from_tm, mod_in, a_send, a_recv, b_send, b_recv, g_send, g_recv, h_send, h_recv, m_send, m_recv,
    k_send, k_recv, head_all, mod_all, mine,
):
    t = lax.axis_index("tm")
    e = lax.axis_index("eval")
    for other in range(n_eval):
        when_not(other == e, lambda: greet((t, other)))
    for other in range(n_tm):
        when_not(other == t, lambda: greet((other, e)))
    pl.semaphore_wait(pltpu.get_barrier_semaphore(), n_eval - 1 + n_tm - 1)

    def eval_peer(d):
        return (e + d) % n_eval

    def tm_peer(d):
        return (t + d) % n_tm

    def head_in(d):
        return remote(head.at[eval_peer(d)], from_eval.at[d - 1], a_send.at[d - 1], a_recv.at[d - 1], (t, eval_peer(d)))

    def mod_scatter(d):
        return remote(mod.at[eval_peer(d)], mod_in.at[d - 1], m_send.at[d - 1], m_recv.at[d - 1], (t, eval_peer(d)))

    for d in range(1, n_eval):
        head_in(d).start()
    for d in range(1, n_eval):
        mod_scatter(d).start()
    part = head[e]
    for d in range(1, n_eval):
        head_in(d).wait_recv()
        part = part + from_eval[d - 1]
    mine[...] = part

    def tm_in(d):
        return remote(mine.at[tm_peer(d)], from_tm.at[d - 1], b_send.at[d - 1], b_recv.at[d - 1], (tm_peer(d), e))

    for d in range(1, n_tm):
        tm_in(d).start()
    mod_sum = mod[e]
    for d in range(1, n_eval):
        mod_scatter(d).wait_recv()
        mod_sum = mod_sum + mod_in[d - 1]
    mod_all[e] = mod_sum

    def mod_spread(d):
        return remote(mod_all.at[e], mod_all.at[e], k_send.at[d - 1], k_recv.at[d - 1], (t, eval_peer(d)))

    for d in range(1, n_eval):
        mod_spread(d).start()
    total = mine[t]
    for d in range(1, n_tm):
        tm_in(d).wait_recv()
        total = total + from_tm[d - 1]
    head_all[e, t] = total

    def tm_spread(d):
        return remote(head_all.at[e, t], head_all.at[e, t], g_send.at[d - 1], g_recv.at[d - 1], (tm_peer(d), e))

    def eval_spread(d):
        return remote(head_all.at[e], head_all.at[e], h_send.at[d - 1], h_recv.at[d - 1], (t, eval_peer(d)))

    for d in range(1, n_tm):
        tm_spread(d).start()
    for d in range(1, n_tm):
        tm_spread(d).wait()
    for d in range(1, n_eval):
        eval_spread(d).start()
    for d in range(1, n_eval):
        head_in(d).wait_send()
        mod_scatter(d).wait_send()
        mod_spread(d).wait()
    for d in range(1, n_tm):
        tm_in(d).wait_send()
    mod_out[...] = mod_all[...]
    for d in range(1, n_eval):
        eval_spread(d).wait()
    head_out[...] = head_all[...]


def params(collective=None):
    if collective is None:
        return pltpu.CompilerParams(vmem_limit_bytes=VMEM_LIMIT)
    return pltpu.CompilerParams(vmem_limit_bytes=VMEM_LIMIT, collective_id=collective, has_side_effects=True)


def per_device(hidden, modulation, head_weight, real_score, fake_score, window_start, timestep):
    fd, tok, width = hidden.shape
    n_tm = lax.axis_size("tm")
    n_eval = lax.axis_size("eval")
    n_win = real_score.shape[0]
    pixel_block = real_score.shape[3]
    n_blk = tok * PATCH // pixel_block
    per = fd // n_eval
    n_x = n_eval // 2
    size = LANES * PATCH
    dma = pltpu.SemaphoreType.DMA
    vmem = pl.BlockSpec(memory_space=pltpu.VMEM)
    smem = pl.BlockSpec(memory_space=pltpu.SMEM)
    by_frame = pl.BlockSpec((1, tok, width), lambda f: (f, 0, 0))
    mod_frame = pl.BlockSpec((1, 2, width), lambda f: (f, 0, 0))
    stat_frame = pl.BlockSpec((1, tok, LANES), lambda f: (f, 0, 0))
    extra_x = max(n_x - 1, 1)

    totals, stats = pl.pallas_call(
        functools.partial(forward_kernel, n_tm, n_eval, n_blk),
        grid=(fd,),
        out_shape=(
            jax.ShapeDtypeStruct((n_win, LANES), F32),
            jax.ShapeDtypeStruct((fd, tok, LANES), F32),
        ),
        in_specs=[smem, by_frame, mod_frame, vmem, vmem],
        out_specs=(pl.BlockSpec((n_win, LANES), lambda f: (0, 0)), stat_frame),
        scratch_shapes=[
            pltpu.VMEM((tok, width), BF16),
            pltpu.VMEM((size, size), BF16),
            pltpu.VMEM((C * PATCH, C * PATCH), BF16),
            pltpu.VMEM((fd, n_blk, C, pixel_block), BF16),
            pltpu.VMEM((n_eval, per, n_tm, C, pixel_block), BF16),
            pltpu.VMEM((n_tm, n_win, LANES), F32),
            dma((fd, n_blk)),
            dma((per, n_tm)),
            dma((per, extra_x)),
            dma((per, extra_x)),
            dma((per, n_x)),
            dma((per, n_x)),
            dma((n_tm - 1,)),
            dma((n_tm - 1,)),
        ],
        compiler_params=params(0),
        name="forward",
    )(window_start, hidden, modulation, head_weight, real_score)

    frames = fd * n_tm
    grad = pl.pallas_call(
        functools.partial(window_kernel, float(WIN * C * pixel_block * n_tm)),
        out_shape=jax.ShapeDtypeStruct((frames, C, pixel_block), F32),
        in_specs=[smem, vmem, vmem, vmem, vmem],
        out_specs=vmem,
        compiler_params=params(),
        name="windows",
    )(window_start, totals, jnp.broadcast_to(timestep[:, None], (n_win, LANES)), real_score, fake_score)

    upstream = pl.pallas_call(
        functools.partial(reduce_kernel, n_tm, n_eval, n_blk),
        out_shape=jax.ShapeDtypeStruct((fd, C, tok * PATCH), BF16),
        in_specs=[vmem],
        out_specs=vmem,
        scratch_shapes=[
            pltpu.VMEM((n_tm, fd // 2, C, pixel_block), F32),
            pltpu.VMEM((n_tm, fd // 2, C, pixel_block), F32),
            pltpu.VMEM((n_tm, extra_x, per, C, pixel_block), F32),
            pltpu.VMEM((n_tm, per, C, pixel_block), BF16),
            pltpu.VMEM((n_blk, n_eval, per, C, pixel_block), BF16),
            dma((n_tm,)),
            dma((n_tm,)),
            dma((n_tm, extra_x)),
            dma((n_tm, extra_x)),
            dma((n_tm,)),
            dma((n_blk, n_eval)),
        ],
        compiler_params=params(1),
        name="reduce",
    )(grad.reshape(n_tm, fd, C, pixel_block))

    d_hidden, head_part, mod_part = pl.pallas_call(
        backward_kernel,
        grid=(fd,),
        out_shape=(
            jax.ShapeDtypeStruct(hidden.shape, BF16),
            jax.ShapeDtypeStruct(head_weight.shape, F32),
            jax.ShapeDtypeStruct((fd, 2, width), F32),
        ),
        in_specs=[
            by_frame,
            mod_frame,
            vmem,
            stat_frame,
            pl.BlockSpec((1, C, tok * PATCH), lambda f: (f, 0, 0)),
        ],
        out_specs=(by_frame, pl.BlockSpec(head_weight.shape, lambda f: (0, 0)), mod_frame),
        scratch_shapes=[
            pltpu.VMEM((tok, width), BF16),
            pltpu.VMEM((tok, width), F32),
            pltpu.VMEM((size, size), BF16),
            pltpu.VMEM((C * PATCH, C * PATCH), BF16),
            pltpu.VMEM((8, width), F32),
            pltpu.VMEM((8, width), F32),
        ],
        compiler_params=params(),
        name="backward",
    )(hidden, modulation, head_weight, stats, upstream)

    head_rows = head_part.size // (n_tm * n_eval * LANES)
    mod_rows = mod_part.size // (n_eval * LANES)
    head_shape = (n_eval, n_tm, head_rows, LANES)
    mod_shape = (n_eval, mod_rows, LANES)
    e_sem, t_sem = dma((n_eval - 1,)), dma((n_tm - 1,))
    head_grad, mod_grad = pl.pallas_call(
        functools.partial(sum_kernel, n_tm, n_eval),
        out_shape=(jax.ShapeDtypeStruct(head_shape, F32), jax.ShapeDtypeStruct(mod_shape, F32)),
        in_specs=[vmem, vmem],
        out_specs=(vmem, vmem),
        scratch_shapes=[
            pltpu.VMEM((n_eval - 1,) + head_shape[1:], F32),
            pltpu.VMEM((n_tm - 1,) + head_shape[2:], F32),
            pltpu.VMEM((n_eval - 1,) + mod_shape[1:], F32),
            e_sem, e_sem, t_sem, t_sem, t_sem, t_sem, e_sem, e_sem, e_sem, e_sem, e_sem, e_sem,
            pltpu.VMEM(head_shape, F32),
            pltpu.VMEM(mod_shape, F32),
            pltpu.VMEM(head_shape[1:], F32),
        ],
        compiler_params=params(2),
        name="sums",
    )(head_part.reshape(head_shape), mod_part.reshape(mod_shape))
    return (d_hidden, head_grad.reshape(head_part.shape), mod_grad.reshape(mod_part.shape))


def solution(mesh):
    placed = (
        P("tm", "eval", None),
        P("tm", None, None),
        P(),
        P("eval", None, None, "tm"),
        P("eval", None, None, "tm"),
        P("eval"),
        P("eval"),
    )
    return jax.shard_map(
        per_device,
        mesh=mesh,
        in_specs=placed,
        out_specs=(P("tm", "eval", None), P(), P("tm", None, None)),
        check_vma=False,
    )
```

```python
import functools

import jax
import jax.numpy as jnp
from jax import lax
from jax.experimental import pallas as pl
from jax.experimental.pallas import tpu as pltpu
from jax.sharding import PartitionSpec as P

C = 16
PATCH = 4
WIN = 21
TOK = 1024
EPS = 1e-06
LANES = 128
ROWS = 16
MESH = pl.DeviceIdType.MESH
VMEM_LIMIT = 56 * 1024 * 1024
F32 = jnp.float32
BF16 = jnp.bfloat16


def remote(src, dst, send_sem, recv_sem, device):
    return pltpu.make_async_remote_copy(
        src_ref=src, dst_ref=dst, send_sem=send_sem, recv_sem=recv_sem, device_id=device, device_id_type=MESH
    )


def greet(device):
    pl.semaphore_signal(pltpu.get_barrier_semaphore(), inc=1, device_id=device, device_id_type=MESH)


def when_not(flag, action):
    pl.when(jnp.logical_not(flag))(action)


def pixel_permutation(inverse):
    size = PATCH * LANES
    lane = lax.broadcasted_iota(jnp.int32, (size, size), 1 if inverse else 0)
    pixel = lax.broadcasted_iota(jnp.int32, (size, size), 0 if inverse else 1)
    return jnp.where(pixel == (lane & (LANES - 1)) * PATCH + (lane >> 7), 1.0, 0.0).astype(BF16)


def row_permutation(inverse):
    size = C * PATCH
    grouped = lax.broadcasted_iota(jnp.int32, (size, size), 1 if inverse else 0)
    mixed = lax.broadcasted_iota(jnp.int32, (size, size), 0 if inverse else 1)
    return jnp.where(mixed == (grouped & (C - 1)) * PATCH + (grouped >> 4), 1.0, 0.0).astype(BF16)


def chunk_rows(i):
    return pl.ds(pl.multiple_of(i * ROWS, ROWS), ROWS)


def dot(a, b, dims=((1,), (0,))):
    return lax.dot_general(a, b, (dims, ((), ())), preferred_element_type=F32)


def forward_kernel(
    n_tm, n_eval, n_blk, starts, hidden, modulation, weight, real, totals, center, inv_std,
    adapted, part, perm, rows, mine, latent, sums, out_send, out_recv, x_send, x_recv, c_send, c_recv, s_send, s_recv,
):
    frame = pl.program_id(0)
    frames = pl.num_programs(0)
    fd = mine.shape[0]
    last = fd - 1
    t = lax.axis_index("tm")
    e = lax.axis_index("eval")
    n_x = n_eval // 2
    x, core = e // 2, e % 2
    partner = 2 * x + 1 - core
    per = fd // n_eval
    tok, width = hidden.shape[1], hidden.shape[2]
    n_win = real.shape[0]

    @pl.when(frame == 0)
    def _():
        source = t // n_blk
        for other in range(n_tm):
            when_not((other == t) & (source == e), lambda: greet((other, source)))
            when_not(other == t, lambda: greet((other, e)))
        for other in range(n_eval):
            when_not(other == e, lambda: greet((t, other)))
        own = jnp.where(source == e, 1, 0)
        pl.semaphore_wait(pltpu.get_barrier_semaphore(), n_tm - own + n_tm - 1 + n_eval - 1)
        perm[...] = pixel_permutation(False)
        rows[...] = row_permutation(False)

    shift = modulation[0, 0:1, :]
    scale = 1.0 + modulation[0, 1:2, :]
    tiles = [slice(i * LANES, (i + 1) * LANES) for i in range(width // LANES)]

    def row_sums(body):
        def step(i, carry):
            at = chunk_rows(i)
            acc = body(at, tiles[0])
            for tile in tiles[1:]:
                acc = acc + body(at, tile)
            part[at, :] = acc
            return carry

        lax.fori_loop(0, tok // ROWS, step, 0, unroll=4)
        return jnp.broadcast_to(jnp.sum(part[...], axis=1, keepdims=True) * (1.0 / width), (tok, LANES))

    def squares(at, tile):
        shifted = hidden[0, at, tile].astype(F32) - center[0, at, :]
        return shifted * shifted

    center[0] = row_sums(lambda at, tile: hidden[0, at, tile].astype(F32))
    inv_std[0] = lax.rsqrt(row_sums(squares) + EPS)

    def adapt(i, carry):
        at = chunk_rows(i)
        for tile in tiles:
            normed = (hidden[0, at, tile].astype(F32) - center[0, at, :]) * inv_std[0, at, :]
            adapted[at, tile] = (normed * scale[:, tile] + shift[:, tile]).astype(BF16)
        return carry

    lax.fori_loop(0, tok // ROWS, adapt, 0, unroll=4)
    out = dot(weight[...], adapted[...], ((1,), (1,))).astype(BF16)
    grouped = dot(rows[...], out).astype(BF16)
    pixels = []
    for j in range(tok // LANES):
        tile = grouped[:, j * LANES : (j + 1) * LANES]
        wide = jnp.concatenate([tile[s * C : (s + 1) * C] for s in range(PATCH)], axis=1)
        pixels.append(dot(wide, perm[...]).astype(BF16))
    pixels = jnp.concatenate(pixels, axis=1)
    pixel_block = mine.shape[3]
    target = frame % n_eval
    place = frame // n_eval
    for b in range(n_blk):
        mine[frame, b] = pixels[:, b * pixel_block : (b + 1) * pixel_block]
    for b in range(n_blk):
        owner = e * n_blk + b
        own = (owner == t) & (target == e)
        dst = latent.at[target, place, t]

        @pl.when(own)
        def _():
            pltpu.make_async_copy(mine.at[frame, b], dst, out_recv.at[place, t]).start()

        @pl.when(jnp.logical_not(own))
        def _():
            remote(mine.at[frame, b], dst, out_send.at[frame, b], out_recv.at[place, t], (owner, target)).start()

    def x_copy(r, d):
        there = 2 * ((x + d) % n_x) + core
        return remote(latent.at[e, r], latent.at[e, r], x_send.at[r, d - 1], x_recv.at[r, d - 1], (t, there))

    def core_copy(r, d):
        held = 2 * ((x + n_x - d) % n_x) + core
        return remote(latent.at[held, r], latent.at[held, r], c_send.at[r, d], c_recv.at[r, d], (t, partner))

    def first(r):
        for source in range(n_tm):
            pltpu.make_async_copy(mine.at[0, 0], latent.at[e, r, source], out_recv.at[r, source]).wait()
        for d in range(1, n_x):
            x_copy(r, d).start()
        core_copy(r, 0).start()

    def second(r):
        for d in range(1, n_x):
            x_copy(r, d).wait_recv()
            core_copy(r, d).start()

    for r in range(per):
        pl.when(frame == min((r + 2) * n_eval - 1, last))(functools.partial(first, r))
    for r in range(per):
        pl.when(frame == min((r + 3) * n_eval - 1, last))(functools.partial(second, r))

    @pl.when(frame == frames - 1)
    def _():
        for f in range(fd):
            for b in range(n_blk):
                owner = e * n_blk + b
                own = (owner == t) & (f % n_eval == e)
                when_not(
                    own,
                    lambda: remote(
                        mine.at[f, b], mine.at[f, b], out_send.at[f, b], out_recv.at[0, 0], (owner, f % n_eval)
                    ).wait_send(),
                )
        for r in range(per):
            for d in range(1, n_x):
                x_copy(r, d).wait_send()
            for d in range(n_x):
                core_copy(r, d).wait()
        row = lax.broadcasted_iota(jnp.int32, (n_win, LANES), 0)
        found = jnp.zeros((n_win, LANES), F32)
        for w in range(n_win):
            start = starts[w]

            def add(k, acc):
                g = start + k
                inner = g % fd
                block = latent[inner % n_eval, inner // n_eval, g // fd].astype(F32)
                return acc + jnp.abs(block - real[w, k].astype(F32))

            acc = lax.fori_loop(0, WIN, add, jnp.zeros(real.shape[2:], F32), unroll=3)
            total = jnp.sum(jnp.sum(acc, axis=0, keepdims=True), axis=1, keepdims=True)
            found = jnp.where(row == w, total, found)
        sums[t] = found
        for d in range(1, n_tm):
            there = (t + d) % n_tm
            remote(sums.at[t], sums.at[t], s_send.at[d - 1], s_recv.at[d - 1], (there, e)).start()
        for d in range(1, n_tm):
            origin = (t + n_tm - d) % n_tm
            remote(sums.at[origin], sums.at[origin], s_send.at[d - 1], s_recv.at[d - 1], (origin, e)).wait()
        result = sums[0]
        for other in range(1, n_tm):
            result = result + sums[other]
        totals[...] = result


def window_kernel(n_pixels, starts, totals, times, real, fake, out):
    out[...] = jnp.zeros_like(out)
    level = times[...].astype(F32) / 1000.0 / (totals[...] / n_pixels + 1e-05)
    for w in range(real.shape[0]):
        start = starts[w]
        gain = level[w : w + 1, 0:1]

        def add(k, carry):
            out[start + k] += gain * (fake[w, k].astype(F32) - real[w, k].astype(F32))
            return carry

        lax.fori_loop(0, WIN, add, 0, unroll=3)


def reduce_kernel(
    n_tm, n_eval, n_blk, grad, out,
    from_core, half, from_x, rounded, landed, c_send, c_recv, x_send, x_recv, o_send, o_recv,
):
    t = lax.axis_index("tm")
    e = lax.axis_index("eval")
    n_x = n_eval // 2
    x, core = e // 2, e % 2
    partner = 2 * x + 1 - core
    fd = grad.shape[1]
    per = fd // n_eval
    mid = fd // 2
    home = t // n_blk
    slot = t % n_blk
    quarter = core * n_x + x

    for other in range(n_eval):
        when_not(other == e, lambda: greet((t, other)))
        for b in range(n_blk):
            when_not((e * n_blk + b == t) & (other == e), lambda: greet((e * n_blk + b, other)))
    own_home = jnp.where(home == e, 1, 0)
    pl.semaphore_wait(pltpu.get_barrier_semaphore(), n_eval - 1 + n_tm - own_home)

    def core_copy(o):
        return remote(
            grad.at[o, pl.ds((1 - core) * mid, mid)], from_core.at[o], c_send.at[o], c_recv.at[o], (t, partner)
        )

    def x_copy(o, d):
        there = (x + d) % n_x
        return remote(
            half.at[o, pl.ds(there * per, per)], from_x.at[o, d - 1], x_send.at[o, d - 1], x_recv.at[o, d - 1],
            (t, 2 * there + core),
        )

    def out_copy(o):
        return remote(
            rounded.at[o], landed.at[slot, quarter], o_send.at[o], o_recv.at[slot, quarter], (o, home)
        )

    def order(i):
        return (t + i) % n_tm

    def start_core(i, carry):
        core_copy(order(i)).start()
        return carry

    def combine(i, carry):
        o = order(i)
        core_copy(o).wait_recv()
        half[o] = grad[o, pl.ds(core * mid, mid)] + from_core[o]
        for d in range(1, n_x):
            x_copy(o, d).start()
        return carry

    def finish(i, carry):
        o = order(i)
        total = half[o, pl.ds(x * per, per)]
        for d in range(1, n_x):
            x_copy(o, d).wait_recv()
            total = total + from_x[o, d - 1]
        rounded[o] = total.astype(BF16)
        own = (o == t) & (home == e)

        @pl.when(own)
        def _():
            pltpu.make_async_copy(rounded.at[o], landed.at[slot, quarter], o_recv.at[slot, quarter]).start()

        @pl.when(jnp.logical_not(own))
        def _():
            out_copy(o).start()

        return carry

    def drain(i, carry):
        o = order(i)
        core_copy(o).wait_send()
        for d in range(1, n_x):
            x_copy(o, d).wait_send()
        when_not((o == t) & (home == e), lambda: out_copy(o).wait_send())
        return carry

    lax.fori_loop(0, n_tm, start_core, 0)
    lax.fori_loop(0, n_tm, combine, 0)
    lax.fori_loop(0, n_tm, finish, 0)
    lax.fori_loop(0, n_tm, drain, 0)
    for b in range(n_blk):
        for q in range(n_eval):
            pltpu.make_async_copy(rounded.at[0], landed.at[b, q], o_recv.at[b, q]).wait()
    pixel_block = grad.shape[3]
    for b in range(n_blk):
        out[:, :, b * pixel_block : (b + 1) * pixel_block] = landed[b].reshape(fd, C, pixel_block)


def backward_kernel(
    hidden, modulation, weight, center, inv_std, upstream, d_hidden, head_tiles, mod_part,
    adapted, d_adapted, perm, rows, head, sum_b, part, mean_a, mean_b,
):
    frame = pl.program_id(0)
    tok, width = hidden.shape[1], hidden.shape[2]

    @pl.when(frame == 0)
    def _():
        perm[...] = pixel_permutation(True)
        rows[...] = row_permutation(True)
        head[...] = jnp.zeros_like(head)

    shift = modulation[0, 0:1, :]
    scale = 1.0 + modulation[0, 1:2, :]
    size = LANES * PATCH
    blocks = []
    for j in range(tok // LANES):
        wide = dot(upstream[0, :, j * size : (j + 1) * size], perm[...]).astype(BF16)
        blocks.append(jnp.concatenate([wide[:, s * LANES : (s + 1) * LANES] for s in range(PATCH)], axis=0))
    up = dot(rows[...], jnp.concatenate(blocks, axis=1)).astype(BF16)
    d_adapted[...] = dot(up, weight[...], ((0,), (0,)))
    weight_f32 = weight[...].astype(F32)
    up_sum = jnp.sum(up.astype(F32), axis=1, keepdims=True)
    mod_part[0, 0:1, :] = jnp.sum(weight_f32 * up_sum, axis=0, keepdims=True)

    level = jnp.sum(weight_f32 * scale, axis=1, keepdims=True) * (1.0 / width)
    rest = jnp.broadcast_to(level, (level.shape[0], LANES))
    total = jnp.zeros((tok, LANES), F32)
    for _ in range(3):
        term = rest.astype(BF16)
        total = total + dot(up, term, ((0,), (0,)))
        rest = rest - term.astype(F32)
    mean_a[...] = total * inv_std[0]
    sum_b[...] = jnp.zeros_like(sum_b)
    tiles = [slice(i * LANES, (i + 1) * LANES) for i in range(width // LANES)]

    def gather(i, carry):
        at = chunk_rows(i)
        acc = jnp.zeros((ROWS, LANES), F32)
        for tile in tiles:
            normed = (hidden[0, at, tile].astype(F32) - center[0, at, :]) * inv_std[0, at, :]
            scaled = normed * scale[:, tile]
            adapted[at, tile] = (scaled + shift[:, tile]).astype(BF16)
            da = d_adapted[at, tile]
            acc = acc + da * scaled
            cross = da * normed
            sum_b[:, tile] += cross[0:8] + cross[8:16]
        part[at, :] = acc
        return carry

    lax.fori_loop(0, tok // ROWS, gather, 0, unroll=4)
    mean_cross = jnp.sum(part[...], axis=1, keepdims=True) * (1.0 / width)
    mean_b[...] = mean_cross * inv_std[0] * inv_std[0]
    head[...] += dot(up, adapted[...])

    def finish(i, carry):
        at = chunk_rows(i)
        for tile in tiles:
            shifted = hidden[0, at, tile].astype(F32) - center[0, at, :]
            dn = d_adapted[at, tile] * scale[:, tile] * inv_std[0, at, :]
            d_hidden[0, at, tile] = (dn - mean_a[at, :] - shifted * mean_b[at, :]).astype(BF16)
        return carry

    lax.fori_loop(0, tok // ROWS, finish, 0, unroll=4)
    mod_part[0, 1:2, :] = jnp.sum(sum_b[...], axis=0, keepdims=True)

    @pl.when(frame == pl.num_programs(0) - 1)
    def _():
        per = head_tiles.shape[2]
        n_tm = head_tiles.shape[1]
        place = 0
        for tile in tiles:
            for r in range(0, head.shape[0], 8):
                head_tiles[place // (per * n_tm), place // per % n_tm, place % per] = head[r : r + 8, tile]
                place += 1
        for place in range(place, head_tiles.shape[0] * n_tm * per):
            head_tiles[place // (per * n_tm), place // per % n_tm, place % per] = jnp.zeros((8, LANES), F32)


def sum_kernel(
    n_tm, n_eval, head, mod, head_out, mod_out,
    from_eval, from_tm, mod_in, a_send, a_recv, b_send, b_recv, g_send, g_recv, h_send, h_recv, m_send, m_recv,
    k_send, k_recv, head_all, mod_all, mine,
):
    t = lax.axis_index("tm")
    e = lax.axis_index("eval")
    for other in range(n_eval):
        when_not(other == e, lambda: greet((t, other)))
    for other in range(n_tm):
        when_not(other == t, lambda: greet((other, e)))
    pl.semaphore_wait(pltpu.get_barrier_semaphore(), n_eval - 1 + n_tm - 1)

    def eval_peer(d):
        return (e + d) % n_eval

    def tm_peer(d):
        return (t + d) % n_tm

    def head_in(d):
        return remote(head.at[eval_peer(d)], from_eval.at[d - 1], a_send.at[d - 1], a_recv.at[d - 1], (t, eval_peer(d)))

    def mod_scatter(d):
        return remote(mod.at[eval_peer(d)], mod_in.at[d - 1], m_send.at[d - 1], m_recv.at[d - 1], (t, eval_peer(d)))

    for d in range(1, n_eval):
        head_in(d).start()
    for d in range(1, n_eval):
        mod_scatter(d).start()
    part = head[e]
    for d in range(1, n_eval):
        head_in(d).wait_recv()
        part = part + from_eval[d - 1]
    mine[...] = part

    def tm_in(d):
        return remote(mine.at[tm_peer(d)], from_tm.at[d - 1], b_send.at[d - 1], b_recv.at[d - 1], (tm_peer(d), e))

    for d in range(1, n_tm):
        tm_in(d).start()
    mod_sum = mod[e]
    for d in range(1, n_eval):
        mod_scatter(d).wait_recv()
        mod_sum = mod_sum + mod_in[d - 1]
    mod_all[e] = mod_sum

    def mod_spread(d):
        return remote(mod_all.at[e], mod_all.at[e], k_send.at[d - 1], k_recv.at[d - 1], (t, eval_peer(d)))

    for d in range(1, n_eval):
        mod_spread(d).start()
    total = mine[t]
    for d in range(1, n_tm):
        tm_in(d).wait_recv()
        total = total + from_tm[d - 1]
    head_all[e, t] = total

    def tm_spread(d):
        return remote(head_all.at[e, t], head_all.at[e, t], g_send.at[d - 1], g_recv.at[d - 1], (tm_peer(d), e))

    def eval_spread(d):
        return remote(head_all.at[e], head_all.at[e], h_send.at[d - 1], h_recv.at[d - 1], (t, eval_peer(d)))

    for d in range(1, n_tm):
        tm_spread(d).start()
    for d in range(1, n_tm):
        tm_spread(d).wait()
    for d in range(1, n_eval):
        eval_spread(d).start()
    for d in range(1, n_eval):
        head_in(d).wait_send()
        mod_scatter(d).wait_send()
        mod_spread(d).wait()
    for d in range(1, n_tm):
        tm_in(d).wait_send()
    mod_out[...] = mod_all[...]
    for d in range(1, n_eval):
        eval_spread(d).wait()
    per = head_all.shape[2]
    place = 0
    for col in range(0, head_out.shape[1], LANES):
        for r in range(0, head_out.shape[0], 8):
            head_out[r : r + 8, col : col + LANES] = head_all[place // (per * n_tm), place // per % n_tm, place % per]
            place += 1


def params(collective=None):
    if collective is None:
        return pltpu.CompilerParams(vmem_limit_bytes=VMEM_LIMIT)
    return pltpu.CompilerParams(vmem_limit_bytes=VMEM_LIMIT, collective_id=collective, has_side_effects=True)


def per_device(hidden, modulation, head_weight, real_score, fake_score, window_start, timestep):
    fd, tok, width = hidden.shape
    n_tm = lax.axis_size("tm")
    n_eval = lax.axis_size("eval")
    n_win = real_score.shape[0]
    pixel_block = real_score.shape[3]
    n_blk = tok * PATCH // pixel_block
    per = fd // n_eval
    n_x = n_eval // 2
    size = LANES * PATCH
    dma = pltpu.SemaphoreType.DMA
    vmem = pl.BlockSpec(memory_space=pltpu.VMEM)
    smem = pl.BlockSpec(memory_space=pltpu.SMEM)
    by_frame = pl.BlockSpec((1, tok, width), lambda f: (f, 0, 0))
    mod_frame = pl.BlockSpec((1, 2, width), lambda f: (f, 0, 0))
    stat_frame = pl.BlockSpec((1, tok, LANES), lambda f: (f, 0, 0))
    extra_x = max(n_x - 1, 1)

    totals, center, inv_std = pl.pallas_call(
        functools.partial(forward_kernel, n_tm, n_eval, n_blk),
        grid=(fd,),
        out_shape=(
            jax.ShapeDtypeStruct((n_win, LANES), F32),
            jax.ShapeDtypeStruct((fd, tok, LANES), F32),
            jax.ShapeDtypeStruct((fd, tok, LANES), F32),
        ),
        in_specs=[smem, by_frame, mod_frame, vmem, vmem],
        out_specs=(pl.BlockSpec((n_win, LANES), lambda f: (0, 0)), stat_frame, stat_frame),
        scratch_shapes=[
            pltpu.VMEM((tok, width), BF16),
            pltpu.VMEM((tok, LANES), F32),
            pltpu.VMEM((size, size), BF16),
            pltpu.VMEM((C * PATCH, C * PATCH), BF16),
            pltpu.VMEM((fd, n_blk, C, pixel_block), BF16),
            pltpu.VMEM((n_eval, per, n_tm, C, pixel_block), BF16),
            pltpu.VMEM((n_tm, n_win, LANES), F32),
            dma((fd, n_blk)),
            dma((per, n_tm)),
            dma((per, extra_x)),
            dma((per, extra_x)),
            dma((per, n_x)),
            dma((per, n_x)),
            dma((n_tm - 1,)),
            dma((n_tm - 1,)),
        ],
        compiler_params=params(0),
        name="forward",
    )(window_start, hidden, modulation, head_weight, real_score)

    frames = fd * n_tm
    grad = pl.pallas_call(
        functools.partial(window_kernel, float(WIN * C * pixel_block * n_tm)),
        out_shape=jax.ShapeDtypeStruct((frames, C, pixel_block), F32),
        in_specs=[smem, vmem, vmem, vmem, vmem],
        out_specs=vmem,
        compiler_params=params(),
        name="windows",
    )(window_start, totals, jnp.broadcast_to(timestep[:, None], (n_win, LANES)), real_score, fake_score)

    upstream = pl.pallas_call(
        functools.partial(reduce_kernel, n_tm, n_eval, n_blk),
        out_shape=jax.ShapeDtypeStruct((fd, C, tok * PATCH), BF16),
        in_specs=[vmem],
        out_specs=vmem,
        scratch_shapes=[
            pltpu.VMEM((n_tm, fd // 2, C, pixel_block), F32),
            pltpu.VMEM((n_tm, fd // 2, C, pixel_block), F32),
            pltpu.VMEM((n_tm, extra_x, per, C, pixel_block), F32),
            pltpu.VMEM((n_tm, per, C, pixel_block), BF16),
            pltpu.VMEM((n_blk, n_eval, per, C, pixel_block), BF16),
            dma((n_tm,)),
            dma((n_tm,)),
            dma((n_tm, extra_x)),
            dma((n_tm, extra_x)),
            dma((n_tm,)),
            dma((n_blk, n_eval)),
        ],
        compiler_params=params(1),
        name="reduce",
    )(grad.reshape(n_tm, fd, C, pixel_block))

    head_tiles = width // LANES * (C * PATCH // 8)
    head_shape = (n_eval, n_tm, pl.cdiv(head_tiles, n_eval * n_tm), 8, LANES)
    d_hidden, head_part, mod_part = pl.pallas_call(
        backward_kernel,
        grid=(fd,),
        out_shape=(
            jax.ShapeDtypeStruct(hidden.shape, BF16),
            jax.ShapeDtypeStruct(head_shape, F32),
            jax.ShapeDtypeStruct((fd, 2, width), F32),
        ),
        in_specs=[
            by_frame,
            mod_frame,
            vmem,
            stat_frame,
            stat_frame,
            pl.BlockSpec((1, C, tok * PATCH), lambda f: (f, 0, 0)),
        ],
        out_specs=(by_frame, pl.BlockSpec(head_shape, lambda f: (0,) * 5), mod_frame),
        scratch_shapes=[
            pltpu.VMEM((tok, width), BF16),
            pltpu.VMEM((tok, width), F32),
            pltpu.VMEM((size, size), BF16),
            pltpu.VMEM((C * PATCH, C * PATCH), BF16),
            pltpu.VMEM((C * PATCH, width), F32),
            pltpu.VMEM((8, width), F32),
            pltpu.VMEM((tok, LANES), F32),
            pltpu.VMEM((tok, LANES), F32),
            pltpu.VMEM((tok, LANES), F32),
        ],
        compiler_params=params(),
        name="backward",
    )(hidden, modulation, head_weight, center, inv_std, upstream)

    mod_shape = (n_eval, per, 2, width)
    e_sem, t_sem = dma((n_eval - 1,)), dma((n_tm - 1,))
    head_grad, mod_grad = pl.pallas_call(
        functools.partial(sum_kernel, n_tm, n_eval),
        out_shape=(jax.ShapeDtypeStruct(head_weight.shape, F32), jax.ShapeDtypeStruct(mod_shape, F32)),
        in_specs=[vmem, vmem],
        out_specs=(vmem, vmem),
        scratch_shapes=[
            pltpu.VMEM((n_eval - 1,) + head_shape[1:], F32),
            pltpu.VMEM((n_tm - 1,) + head_shape[2:], F32),
            pltpu.VMEM((n_eval - 1,) + mod_shape[1:], F32),
            e_sem, e_sem, t_sem, t_sem, t_sem, t_sem, e_sem, e_sem, e_sem, e_sem, e_sem, e_sem,
            pltpu.VMEM(head_shape, F32),
            pltpu.VMEM(mod_shape, F32),
            pltpu.VMEM(head_shape[1:], F32),
        ],
        compiler_params=params(2),
        name="sums",
    )(head_part, mod_part.reshape(mod_shape))
    return (d_hidden, head_grad, mod_grad.reshape(mod_part.shape))


def solution(mesh):
    placed = (
        P("tm", "eval", None),
        P("tm", None, None),
        P(),
        P("eval", None, None, "tm"),
        P("eval", None, None, "tm"),
        P("eval"),
        P("eval"),
    )
    return jax.shard_map(
        per_device,
        mesh=mesh,
        in_specs=placed,
        out_specs=(P("tm", "eval", None), P(), P("tm", None, None)),
        check_vma=False,
    )
```

```python
import functools

import jax
import jax.numpy as jnp
from jax import lax
from jax.experimental import pallas as pl
from jax.experimental.pallas import tpu as pltpu
from jax.sharding import PartitionSpec as P

C = 16
PATCH = 4
WIN = 21
TOK = 1024
EPS = 1e-06
LANES = 128
ROWS = 32
SUB = 8
PAIR = 2
MESH = pl.DeviceIdType.MESH
VMEM_LIMIT = 56 * 1024 * 1024
F32 = jnp.float32
BF16 = jnp.bfloat16


def remote(src, dst, send_sem, recv_sem, device):
    return pltpu.make_async_remote_copy(
        src_ref=src, dst_ref=dst, send_sem=send_sem, recv_sem=recv_sem, device_id=device, device_id_type=MESH
    )


def greet(device):
    pl.semaphore_signal(pltpu.get_barrier_semaphore(), inc=1, device_id=device, device_id_type=MESH)


def when_not(flag, action):
    pl.when(jnp.logical_not(flag))(action)


def pixel_permutation(inverse):
    size = PATCH * LANES
    lane = lax.broadcasted_iota(jnp.int32, (size, size), 1 if inverse else 0)
    pixel = lax.broadcasted_iota(jnp.int32, (size, size), 0 if inverse else 1)
    return jnp.where(pixel == (lane & (LANES - 1)) * PATCH + (lane >> 7), 1.0, 0.0).astype(BF16)


def row_permutation(inverse):
    size = C * PATCH
    grouped = lax.broadcasted_iota(jnp.int32, (size, size), 1 if inverse else 0)
    mixed = lax.broadcasted_iota(jnp.int32, (size, size), 0 if inverse else 1)
    return jnp.where(mixed == (grouped & (C - 1)) * PATCH + (grouped >> 4), 1.0, 0.0).astype(BF16)


def chunk_rows(i):
    return pl.ds(pl.multiple_of(i * ROWS, ROWS), ROWS)


def by_sublane(block):
    return block.reshape(block.shape[0] // SUB, SUB, block.shape[1])


def dot(a, b, dims=((1,), (0,))):
    return lax.dot_general(a, b, (dims, ((), ())), preferred_element_type=F32)


def forward_kernel(
    n_tm, n_eval, n_blk, starts, hidden, modulation, weight, real, totals, center, inv_std,
    adapted, part, shift8, scale8, perm, rows, mine, latent, sums, out_send, out_recv, x_send, x_recv, c_send, c_recv, s_send, s_recv,
):
    frame = pl.program_id(0)
    frames = pl.num_programs(0)
    fd = mine.shape[0]
    last = fd - 1
    t = lax.axis_index("tm")
    e = lax.axis_index("eval")
    n_x = n_eval // 2
    x, core = e // 2, e % 2
    partner = 2 * x + 1 - core
    per = fd // n_eval
    tok, width = hidden.shape[1], hidden.shape[2]
    n_win = real.shape[0]

    @pl.when(frame == 0)
    def _():
        source = t // n_blk
        for other in range(n_tm):
            when_not((other == t) & (source == e), lambda: greet((other, source)))
            when_not(other == t, lambda: greet((other, e)))
        for other in range(n_eval):
            when_not(other == e, lambda: greet((t, other)))
        own = jnp.where(source == e, 1, 0)
        pl.semaphore_wait(pltpu.get_barrier_semaphore(), n_tm - own + n_tm - 1 + n_eval - 1)
        perm[...] = pixel_permutation(False)
        rows[...] = row_permutation(False)

    tiles = [slice(i * LANES, (i + 1) * LANES) for i in range(width // LANES)]
    shift8[...] = jnp.broadcast_to(modulation[0, 0:1, :], shift8.shape)
    scale8[...] = jnp.broadcast_to(1.0 + modulation[0, 1:2, :], scale8.shape)

    def row_sums(body):
        def step(i, carry):
            at = chunk_rows(i)
            add_tile = body(at)
            acc = add_tile(tiles[0])
            for tile in tiles[1:]:
                acc = acc + add_tile(tile)
            part[at, :] = acc
            return carry

        lax.fori_loop(0, tok // ROWS, step, 0, unroll=2)
        return jnp.broadcast_to(jnp.sum(part[...], axis=1, keepdims=True) * (1.0 / width), (tok, LANES))

    def squares(at):
        middle = center[0, at, :]

        def body(tile):
            shifted = hidden[0, at, tile].astype(F32) - middle
            return shifted * shifted

        return body

    center[0] = row_sums(lambda at: lambda tile: hidden[0, at, tile].astype(F32))
    inv_std[0] = lax.rsqrt(row_sums(squares) + EPS)
    turn = frame % PAIR

    def adapt(i, carry):
        at = chunk_rows(i)
        middle, inv = center[0, at, :], inv_std[0, at, :]
        for tile in tiles:
            normed = by_sublane((hidden[0, at, tile].astype(F32) - middle) * inv)
            shaped = normed * scale8[:, tile] + shift8[:, tile]
            adapted[turn, at, tile] = shaped.reshape(ROWS, LANES).astype(BF16)
        return carry

    lax.fori_loop(0, tok // ROWS, adapt, 0, unroll=2)

    @pl.when(turn == PAIR - 1)
    def _():
        out = dot(weight[...], adapted[...].reshape(PAIR * tok, width), ((1,), (1,))).astype(BF16)
        grouped = dot(rows[...], out).astype(BF16)
        wide = []
        for j in range(PAIR * tok // LANES):
            tile = grouped[:, j * LANES : (j + 1) * LANES]
            wide.append(jnp.concatenate([tile[s * C : (s + 1) * C] for s in range(PATCH)], axis=1))
        pixels = dot(jnp.concatenate(wide, axis=0), perm[...]).astype(BF16)
        pixel_block = mine.shape[3]
        per_tile = PATCH * LANES // pixel_block
        for p in range(PAIR):
            f = frame - (PAIR - 1) + p
            target = f % n_eval
            place = f // n_eval
            for b in range(n_blk):
                row = (p * (tok // LANES) + b // per_tile) * C
                col = b % per_tile * pixel_block
                mine[f, b] = pixels[row : row + C, col : col + pixel_block]
            for b in range(n_blk):
                owner = e * n_blk + b
                own = (owner == t) & (target == e)
                dst = latent.at[target, place, t]

                @pl.when(own)
                def _():
                    pltpu.make_async_copy(mine.at[f, b], dst, out_recv.at[place, t]).start()

                @pl.when(jnp.logical_not(own))
                def _():
                    remote(mine.at[f, b], dst, out_send.at[f, b], out_recv.at[place, t], (owner, target)).start()

    def x_copy(r, d):
        there = 2 * ((x + d) % n_x) + core
        return remote(latent.at[e, r], latent.at[e, r], x_send.at[r, d - 1], x_recv.at[r, d - 1], (t, there))

    def core_copy(r, d):
        held = 2 * ((x + n_x - d) % n_x) + core
        return remote(latent.at[held, r], latent.at[held, r], c_send.at[r, d], c_recv.at[r, d], (t, partner))

    def first(r):
        for source in range(n_tm):
            pltpu.make_async_copy(mine.at[0, 0], latent.at[e, r, source], out_recv.at[r, source]).wait()
        for d in range(1, n_x):
            x_copy(r, d).start()
        core_copy(r, 0).start()

    def second(r):
        for d in range(1, n_x):
            x_copy(r, d).wait_recv()
            core_copy(r, d).start()

    for r in range(per):
        pl.when(frame == min((r + 2) * n_eval - 1, last))(functools.partial(first, r))
    for r in range(per):
        pl.when(frame == min((r + 3) * n_eval - 1, last))(functools.partial(second, r))

    @pl.when(frame == frames - 1)
    def _():
        for f in range(fd):
            for b in range(n_blk):
                owner = e * n_blk + b
                own = (owner == t) & (f % n_eval == e)
                when_not(
                    own,
                    lambda: remote(
                        mine.at[f, b], mine.at[f, b], out_send.at[f, b], out_recv.at[0, 0], (owner, f % n_eval)
                    ).wait_send(),
                )
        for r in range(per):
            for d in range(1, n_x):
                x_copy(r, d).wait_send()
            for d in range(n_x):
                core_copy(r, d).wait()
        row = lax.broadcasted_iota(jnp.int32, (n_win, LANES), 0)
        found = jnp.zeros((n_win, LANES), F32)
        for w in range(n_win):
            start = starts[w]

            def add(k, acc):
                g = start + k
                inner = g % fd
                block = latent[inner % n_eval, inner // n_eval, g // fd].astype(F32)
                return acc + jnp.abs(block - real[w, k].astype(F32))

            acc = lax.fori_loop(0, WIN, add, jnp.zeros(real.shape[2:], F32), unroll=3)
            total = jnp.sum(jnp.sum(acc, axis=0, keepdims=True), axis=1, keepdims=True)
            found = jnp.where(row == w, total, found)
        sums[t] = found
        for d in range(1, n_tm):
            there = (t + d) % n_tm
            remote(sums.at[t], sums.at[t], s_send.at[d - 1], s_recv.at[d - 1], (there, e)).start()
        for d in range(1, n_tm):
            origin = (t + n_tm - d) % n_tm
            remote(sums.at[origin], sums.at[origin], s_send.at[d - 1], s_recv.at[d - 1], (origin, e)).wait()
        result = sums[0]
        for other in range(1, n_tm):
            result = result + sums[other]
        totals[...] = result


def reduce_kernel(
    n_tm, n_eval, n_blk, starts, times, totals, real, fake, out,
    grad, gain, from_core, half, from_x, rounded, landed, c_send, c_recv, x_send, x_recv, o_send, o_recv,
):
    t = lax.axis_index("tm")
    e = lax.axis_index("eval")
    n_x = n_eval // 2
    x, core = e // 2, e % 2
    partner = 2 * x + 1 - core
    fd = grad.shape[1]
    per = fd // n_eval
    mid = fd // 2
    home = t // n_blk
    slot = t % n_blk
    quarter = core * n_x + x

    for other in range(n_eval):
        when_not(other == e, lambda: greet((t, other)))
        for b in range(n_blk):
            when_not((e * n_blk + b == t) & (other == e), lambda: greet((e * n_blk + b, other)))
    own_home = jnp.where(home == e, 1, 0)
    pl.semaphore_wait(pltpu.get_barrier_semaphore(), n_eval - 1 + n_tm - own_home)

    def core_copy(o):
        return remote(
            grad.at[o, pl.ds((1 - core) * mid, mid)], from_core.at[o], c_send.at[o], c_recv.at[o], (t, partner)
        )

    def x_copy(o, d):
        there = (x + d) % n_x
        return remote(
            half.at[o, pl.ds(there * per, per)], from_x.at[o, d - 1], x_send.at[o, d - 1], x_recv.at[o, d - 1],
            (t, 2 * there + core),
        )

    def out_copy(o):
        return remote(
            rounded.at[o], landed.at[slot, quarter], o_send.at[o], o_recv.at[slot, quarter], (o, home)
        )

    def order(i):
        return (t + i) % n_tm

    pixel_block = grad.shape[3]
    n_win = real.shape[0]
    spread = totals[...] / float(WIN * C * pixel_block * n_tm) + 1e-05
    for w in range(n_win):
        level = times[w].astype(F32) / 1000.0
        gain[w] = jnp.broadcast_to(level / spread[w : w + 1, :], (SUB, LANES))

    def start_core(i):
        o = order(i)

        def build(j, carry):
            total = jnp.zeros((C, pixel_block), F32)
            for w in range(n_win):
                k = o * fd + j - starts[w]
                inside = jnp.where((k >= 0) & (k < WIN), 1.0, 0.0)
                k = jnp.clip(k, 0, WIN - 1)
                factor = gain[w] * inside
                factor = jnp.concatenate([factor] * (pixel_block // LANES), axis=1)
                factor = jnp.concatenate([factor] * (C // SUB), axis=0)
                total = total + factor * (fake[w, k].astype(F32) - real[w, k].astype(F32))
            grad[o, j] = total
            return carry

        lax.fori_loop(0, fd, build, 0)
        core_copy(o).start()

    def combine(i):
        o = order(i)
        core_copy(o).wait_recv()
        half[o] = grad[o, pl.ds(core * mid, mid)] + from_core[o]
        for d in range(1, n_x):
            x_copy(o, d).start()

    def finish(i):
        o = order(i)
        total = half[o, pl.ds(x * per, per)]
        for d in range(1, n_x):
            x_copy(o, d).wait_recv()
            total = total + from_x[o, d - 1]
        rounded[o] = total.astype(BF16)
        own = (o == t) & (home == e)

        @pl.when(own)
        def _():
            pltpu.make_async_copy(rounded.at[o], landed.at[slot, quarter], o_recv.at[slot, quarter]).start()

        @pl.when(jnp.logical_not(own))
        def _():
            out_copy(o).start()

    def drain(i, carry):
        o = order(i)
        core_copy(o).wait_send()
        for d in range(1, n_x):
            x_copy(o, d).wait_send()
        when_not((o == t) & (home == e), lambda: out_copy(o).wait_send())
        return carry

    lag = min(4, n_tm)

    def step(i, carry):
        pl.when(i < n_tm)(lambda: start_core(i))
        pl.when((i >= 1) & (i < n_tm + 1))(lambda: combine(i - 1))
        pl.when(i >= lag)(lambda: finish(i - lag))
        return carry

    lax.fori_loop(0, n_tm + lag, step, 0)
    lax.fori_loop(0, n_tm, drain, 0)
    for b in range(n_blk):
        for q in range(n_eval):
            pltpu.make_async_copy(rounded.at[0], landed.at[b, q], o_recv.at[b, q]).wait()
    for b in range(n_blk):
        out[:, :, b * pixel_block : (b + 1) * pixel_block] = landed[b].reshape(fd, C, pixel_block)


def backward_kernel(
    hidden, modulation, weight, center, inv_std, upstream, d_hidden, head_tiles, mod_part,
    adapted, d_adapted, ups, shift8, scale8, perm, rows, head, sum_b, part, mean_a, mean_b,
):
    frame = pl.program_id(0)
    tok, width = hidden.shape[1], hidden.shape[2]

    @pl.when(frame == 0)
    def _():
        perm[...] = pixel_permutation(True)
        rows[...] = row_permutation(True)
        head[...] = jnp.zeros_like(head)
        size = LANES * PATCH
        fd = ups.shape[0]
        flat = upstream[...].reshape(fd * C, tok * PATCH)
        for j in range(tok // LANES):
            wide = dot(flat[:, j * size : (j + 1) * size], perm[...]).astype(BF16)
            for f in range(fd):
                block = [wide[f * C : (f + 1) * C, s * LANES : (s + 1) * LANES] for s in range(PATCH)]
                ups[f, :, j * LANES : (j + 1) * LANES] = jnp.concatenate(block, axis=0)
        mixed = dot(rows[...], jnp.concatenate([ups[f] for f in range(fd)], axis=1)).astype(BF16)
        for f in range(fd):
            ups[f] = mixed[:, f * tok : (f + 1) * tok]

    scale = 1.0 + modulation[0, 1:2, :]
    shift8[...] = jnp.broadcast_to(modulation[0, 0:1, :], shift8.shape)
    scale8[...] = jnp.broadcast_to(scale, scale8.shape)
    up = ups[frame]
    d_adapted[...] = dot(up, weight[...], ((0,), (0,)))
    weight_f32 = weight[...].astype(F32)
    up_sum = jnp.sum(up.astype(F32), axis=1, keepdims=True)
    mod_part[0, 0:1, :] = jnp.sum(weight_f32 * up_sum, axis=0, keepdims=True)

    level = jnp.sum(weight_f32 * scale, axis=1, keepdims=True) * (1.0 / width)
    rest = jnp.broadcast_to(level, (level.shape[0], LANES))
    total = jnp.zeros((tok, LANES), F32)
    for _ in range(3):
        term = rest.astype(BF16)
        total = total + dot(up, term, ((0,), (0,)))
        rest = rest - term.astype(F32)
    mean_a[...] = total * inv_std[0]
    sum_b[...] = jnp.zeros_like(sum_b)
    tiles = [slice(i * LANES, (i + 1) * LANES) for i in range(width // LANES)]

    def gather(i, carry):
        at = chunk_rows(i)
        middle, inv = center[0, at, :], inv_std[0, at, :]
        acc = jnp.zeros((ROWS // SUB, SUB, LANES), F32)
        for tile in tiles:
            normed = by_sublane((hidden[0, at, tile].astype(F32) - middle) * inv)
            scaled = normed * scale8[:, tile]
            adapted[at, tile] = (scaled + shift8[:, tile]).reshape(ROWS, LANES).astype(BF16)
            da = by_sublane(d_adapted[at, tile])
            acc = acc + da * scaled
            sum_b[:, tile] += jnp.sum(da * normed, axis=0)
        part[at, :] = acc.reshape(ROWS, LANES)
        return carry

    lax.fori_loop(0, tok // ROWS, gather, 0, unroll=2)
    mean_cross = jnp.sum(part[...], axis=1, keepdims=True) * (1.0 / width)
    mean_b[...] = mean_cross * inv_std[0] * inv_std[0]
    head[...] += dot(up, adapted[...])

    def finish(i, carry):
        at = chunk_rows(i)
        middle, inv, first, second = center[0, at, :], inv_std[0, at, :], mean_a[at, :], mean_b[at, :]
        for tile in tiles:
            shifted = hidden[0, at, tile].astype(F32) - middle
            dn = (by_sublane(d_adapted[at, tile]) * scale8[:, tile]).reshape(ROWS, LANES) * inv
            d_hidden[0, at, tile] = (dn - first - shifted * second).astype(BF16)
        return carry

    lax.fori_loop(0, tok // ROWS, finish, 0, unroll=2)
    mod_part[0, 1:2, :] = jnp.sum(sum_b[...], axis=0, keepdims=True)

    @pl.when(frame == pl.num_programs(0) - 1)
    def _():
        per = head_tiles.shape[2]
        n_tm = head_tiles.shape[1]
        place = 0
        for tile in tiles:
            for r in range(0, head.shape[0], 8):
                head_tiles[place // (per * n_tm), place // per % n_tm, place % per] = head[r : r + 8, tile]
                place += 1
        for place in range(place, head_tiles.shape[0] * n_tm * per):
            head_tiles[place // (per * n_tm), place // per % n_tm, place % per] = jnp.zeros((8, LANES), F32)


def sum_kernel(
    n_tm, n_eval, head, mod, head_out, mod_out,
    from_eval, from_tm, mod_in, a_send, a_recv, b_send, b_recv, g_send, g_recv, h_send, h_recv, m_send, m_recv,
    k_send, k_recv, head_all, mod_all, mine,
):
    t = lax.axis_index("tm")
    e = lax.axis_index("eval")
    for other in range(n_eval):
        when_not(other == e, lambda: greet((t, other)))
    for other in range(n_tm):
        when_not(other == t, lambda: greet((other, e)))
    pl.semaphore_wait(pltpu.get_barrier_semaphore(), n_eval - 1 + n_tm - 1)

    def eval_peer(d):
        return (e + d) % n_eval

    def tm_peer(d):
        return (t + d) % n_tm

    def head_in(d):
        return remote(head.at[eval_peer(d)], from_eval.at[d - 1], a_send.at[d - 1], a_recv.at[d - 1], (t, eval_peer(d)))

    def mod_scatter(d):
        return remote(mod.at[eval_peer(d)], mod_in.at[d - 1], m_send.at[d - 1], m_recv.at[d - 1], (t, eval_peer(d)))

    for d in range(1, n_eval):
        head_in(d).start()
    for d in range(1, n_eval):
        mod_scatter(d).start()
    part = head[e]
    for d in range(1, n_eval):
        head_in(d).wait_recv()
        part = part + from_eval[d - 1]
    mine[...] = part

    def tm_in(d):
        return remote(mine.at[tm_peer(d)], from_tm.at[d - 1], b_send.at[d - 1], b_recv.at[d - 1], (tm_peer(d), e))

    for d in range(1, n_tm):
        tm_in(d).start()
    mod_sum = mod[e]
    for d in range(1, n_eval):
        mod_scatter(d).wait_recv()
        mod_sum = mod_sum + mod_in[d - 1]
    mod_all[e] = mod_sum

    def mod_spread(d):
        return remote(mod_all.at[e], mod_all.at[e], k_send.at[d - 1], k_recv.at[d - 1], (t, eval_peer(d)))

    for d in range(1, n_eval):
        mod_spread(d).start()
    total = mine[t]
    for d in range(1, n_tm):
        tm_in(d).wait_recv()
        total = total + from_tm[d - 1]
    head_all[e, t] = total

    def tm_spread(d):
        return remote(head_all.at[e, t], head_all.at[e, t], g_send.at[d - 1], g_recv.at[d - 1], (tm_peer(d), e))

    def eval_spread(d):
        return remote(head_all.at[e], head_all.at[e], h_send.at[d - 1], h_recv.at[d - 1], (t, eval_peer(d)))

    for d in range(1, n_tm):
        tm_spread(d).start()
    for d in range(1, n_tm):
        tm_spread(d).wait()
    for d in range(1, n_eval):
        eval_spread(d).start()
    for d in range(1, n_eval):
        head_in(d).wait_send()
        mod_scatter(d).wait_send()
        mod_spread(d).wait()
    for d in range(1, n_tm):
        tm_in(d).wait_send()
    mod_out[...] = mod_all[...]
    for d in range(1, n_eval):
        eval_spread(d).wait()
    per = head_all.shape[2]
    place = 0
    for col in range(0, head_out.shape[1], LANES):
        for r in range(0, head_out.shape[0], 8):
            head_out[r : r + 8, col : col + LANES] = head_all[place // (per * n_tm), place // per % n_tm, place % per]
            place += 1


def params(collective=None):
    if collective is None:
        return pltpu.CompilerParams(vmem_limit_bytes=VMEM_LIMIT)
    return pltpu.CompilerParams(vmem_limit_bytes=VMEM_LIMIT, collective_id=collective, has_side_effects=True)


def per_device(hidden, modulation, head_weight, real_score, fake_score, window_start, timestep):
    fd, tok, width = hidden.shape
    n_tm = lax.axis_size("tm")
    n_eval = lax.axis_size("eval")
    n_win = real_score.shape[0]
    pixel_block = real_score.shape[3]
    n_blk = tok * PATCH // pixel_block
    per = fd // n_eval
    n_x = n_eval // 2
    size = LANES * PATCH
    dma = pltpu.SemaphoreType.DMA
    vmem = pl.BlockSpec(memory_space=pltpu.VMEM)
    smem = pl.BlockSpec(memory_space=pltpu.SMEM)
    by_frame = pl.BlockSpec((1, tok, width), lambda f: (f, 0, 0))
    mod_frame = pl.BlockSpec((1, 2, width), lambda f: (f, 0, 0))
    stat_frame = pl.BlockSpec((1, tok, LANES), lambda f: (f, 0, 0))
    extra_x = max(n_x - 1, 1)

    totals, center, inv_std = pl.pallas_call(
        functools.partial(forward_kernel, n_tm, n_eval, n_blk),
        grid=(fd,),
        out_shape=(
            jax.ShapeDtypeStruct((n_win, LANES), F32),
            jax.ShapeDtypeStruct((fd, tok, LANES), F32),
            jax.ShapeDtypeStruct((fd, tok, LANES), F32),
        ),
        in_specs=[smem, by_frame, mod_frame, vmem, vmem],
        out_specs=(pl.BlockSpec((n_win, LANES), lambda f: (0, 0)), stat_frame, stat_frame),
        scratch_shapes=[
            pltpu.VMEM((PAIR, tok, width), BF16),
            pltpu.VMEM((tok, LANES), F32),
            pltpu.VMEM((SUB, width), F32),
            pltpu.VMEM((SUB, width), F32),
            pltpu.VMEM((size, size), BF16),
            pltpu.VMEM((C * PATCH, C * PATCH), BF16),
            pltpu.VMEM((fd, n_blk, C, pixel_block), BF16),
            pltpu.VMEM((n_eval, per, n_tm, C, pixel_block), BF16),
            pltpu.VMEM((n_tm, n_win, LANES), F32),
            dma((fd, n_blk)),
            dma((per, n_tm)),
            dma((per, extra_x)),
            dma((per, extra_x)),
            dma((per, n_x)),
            dma((per, n_x)),
            dma((n_tm - 1,)),
            dma((n_tm - 1,)),
        ],
        compiler_params=params(0),
        name="forward",
    )(window_start, hidden, modulation, head_weight, real_score)

    upstream = pl.pallas_call(
        functools.partial(reduce_kernel, n_tm, n_eval, n_blk),
        out_shape=jax.ShapeDtypeStruct((fd, C, tok * PATCH), BF16),
        in_specs=[smem, smem, vmem, vmem, vmem],
        out_specs=vmem,
        scratch_shapes=[
            pltpu.VMEM((n_tm, fd, C, pixel_block), F32),
            pltpu.VMEM((n_win, SUB, LANES), F32),
            pltpu.VMEM((n_tm, fd // 2, C, pixel_block), F32),
            pltpu.VMEM((n_tm, fd // 2, C, pixel_block), F32),
            pltpu.VMEM((n_tm, extra_x, per, C, pixel_block), F32),
            pltpu.VMEM((n_tm, per, C, pixel_block), BF16),
            pltpu.VMEM((n_blk, n_eval, per, C, pixel_block), BF16),
            dma((n_tm,)),
            dma((n_tm,)),
            dma((n_tm, extra_x)),
            dma((n_tm, extra_x)),
            dma((n_tm,)),
            dma((n_blk, n_eval)),
        ],
        compiler_params=params(1),
        name="reduce",
    )(window_start, timestep, totals, real_score, fake_score)

    head_tiles = width // LANES * (C * PATCH // 8)
    head_shape = (n_eval, n_tm, pl.cdiv(head_tiles, n_eval * n_tm), 8, LANES)
    d_hidden, head_part, mod_part = pl.pallas_call(
        backward_kernel,
        grid=(fd,),
        out_shape=(
            jax.ShapeDtypeStruct(hidden.shape, BF16),
            jax.ShapeDtypeStruct(head_shape, F32),
            jax.ShapeDtypeStruct((fd, 2, width), F32),
        ),
        in_specs=[
            by_frame,
            mod_frame,
            vmem,
            stat_frame,
            stat_frame,
            vmem,
        ],
        out_specs=(by_frame, pl.BlockSpec(head_shape, lambda f: (0,) * 5), mod_frame),
        scratch_shapes=[
            pltpu.VMEM((tok, width), BF16),
            pltpu.VMEM((tok, width), F32),
            pltpu.VMEM((fd, C * PATCH, tok), BF16),
            pltpu.VMEM((SUB, width), F32),
            pltpu.VMEM((SUB, width), F32),
            pltpu.VMEM((size, size), BF16),
            pltpu.VMEM((C * PATCH, C * PATCH), BF16),
            pltpu.VMEM((C * PATCH, width), F32),
            pltpu.VMEM((8, width), F32),
            pltpu.VMEM((tok, LANES), F32),
            pltpu.VMEM((tok, LANES), F32),
            pltpu.VMEM((tok, LANES), F32),
        ],
        compiler_params=params(),
        name="backward",
    )(hidden, modulation, head_weight, center, inv_std, upstream)

    mod_shape = (n_eval, per, 2, width)
    e_sem, t_sem = dma((n_eval - 1,)), dma((n_tm - 1,))
    head_grad, mod_grad = pl.pallas_call(
        functools.partial(sum_kernel, n_tm, n_eval),
        out_shape=(jax.ShapeDtypeStruct(head_weight.shape, F32), jax.ShapeDtypeStruct(mod_shape, F32)),
        in_specs=[vmem, vmem],
        out_specs=(vmem, vmem),
        scratch_shapes=[
            pltpu.VMEM((n_eval - 1,) + head_shape[1:], F32),
            pltpu.VMEM((n_tm - 1,) + head_shape[2:], F32),
            pltpu.VMEM((n_eval - 1,) + mod_shape[1:], F32),
            e_sem, e_sem, t_sem, t_sem, t_sem, t_sem, e_sem, e_sem, e_sem, e_sem, e_sem, e_sem,
            pltpu.VMEM(head_shape, F32),
            pltpu.VMEM(mod_shape, F32),
            pltpu.VMEM(head_shape[1:], F32),
        ],
        compiler_params=params(2),
        name="sums",
    )(head_part, mod_part.reshape(mod_shape))
    return (d_hidden, head_grad, mod_grad.reshape(mod_part.shape))


def solution(mesh):
    placed = (
        P("tm", "eval", None),
        P("tm", None, None),
        P(),
        P("eval", None, None, "tm"),
        P("eval", None, None, "tm"),
        P("eval"),
        P("eval"),
    )
    return jax.shard_map(
        per_device,
        mesh=mesh,
        in_specs=placed,
        out_specs=(P("tm", "eval", None), P(), P("tm", None, None)),
        check_vma=False,
    )
```

```python
import functools

import jax
import jax.numpy as jnp
from jax import lax
from jax.experimental import pallas as pl
from jax.experimental.pallas import tpu as pltpu
from jax.sharding import PartitionSpec as P

C = 16
PATCH = 4
WIN = 21
TOK = 1024
EPS = 1e-06
LANES = 128
ROWS = 32
SUB = 8
PAIR = 2
LAG = 5
MESH = pl.DeviceIdType.MESH
VMEM_LIMIT = 56 * 1024 * 1024
F32 = jnp.float32
BF16 = jnp.bfloat16


def remote(src, dst, send_sem, recv_sem, device):
    return pltpu.make_async_remote_copy(
        src_ref=src, dst_ref=dst, send_sem=send_sem, recv_sem=recv_sem, device_id=device, device_id_type=MESH
    )


def greet(device):
    pl.semaphore_signal(pltpu.get_barrier_semaphore(), inc=1, device_id=device, device_id_type=MESH)


def when_not(flag, action):
    pl.when(jnp.logical_not(flag))(action)


def pixel_permutation(inverse):
    size = PATCH * LANES
    lane = lax.broadcasted_iota(jnp.int32, (size, size), 1 if inverse else 0)
    pixel = lax.broadcasted_iota(jnp.int32, (size, size), 0 if inverse else 1)
    return jnp.where(pixel == (lane & (LANES - 1)) * PATCH + (lane >> 7), 1.0, 0.0).astype(BF16)


def row_permutation(inverse):
    size = C * PATCH
    grouped = lax.broadcasted_iota(jnp.int32, (size, size), 1 if inverse else 0)
    mixed = lax.broadcasted_iota(jnp.int32, (size, size), 0 if inverse else 1)
    return jnp.where(mixed == (grouped & (C - 1)) * PATCH + (grouped >> 4), 1.0, 0.0).astype(BF16)


def chunk_rows(i):
    return pl.ds(pl.multiple_of(i * ROWS, ROWS), ROWS)


def by_sublane(block):
    return block.reshape(block.shape[0] // SUB, SUB, block.shape[1])


def dot(a, b, dims=((1,), (0,))):
    return lax.dot_general(a, b, (dims, ((), ())), preferred_element_type=F32)


def forward_kernel(
    n_tm, n_eval, n_blk, starts, hidden, modulation, weight, real, totals, center, inv_std,
    adapted, part, shift8, scale8, perm, rows, mine, latent, sums, out_send, out_recv, x_send, x_recv, c_send, c_recv, s_send, s_recv,
):
    frame = pl.program_id(0)
    frames = pl.num_programs(0)
    fd = mine.shape[0]
    last = fd - 1
    t = lax.axis_index("tm")
    e = lax.axis_index("eval")
    n_x = n_eval // 2
    x, core = e // 2, e % 2
    partner = 2 * x + 1 - core
    per = fd // n_eval
    tok, width = hidden.shape[1], hidden.shape[2]
    n_win = real.shape[0]

    @pl.when(frame == 0)
    def _():
        source = t // n_blk
        for other in range(n_tm):
            when_not((other == t) & (source == e), lambda: greet((other, source)))
            when_not(other == t, lambda: greet((other, e)))
        for other in range(n_eval):
            when_not(other == e, lambda: greet((t, other)))
        own = jnp.where(source == e, 1, 0)
        pl.semaphore_wait(pltpu.get_barrier_semaphore(), n_tm - own + n_tm - 1 + n_eval - 1)
        perm[...] = pixel_permutation(False)
        rows[...] = row_permutation(False)

    tiles = [slice(i * LANES, (i + 1) * LANES) for i in range(width // LANES)]
    shift8[...] = jnp.broadcast_to(modulation[0, 0:1, :], shift8.shape)
    scale8[...] = jnp.broadcast_to(1.0 + modulation[0, 1:2, :], scale8.shape)

    def row_sums(body):
        def step(i, carry):
            at = chunk_rows(i)
            add_tile = body(at)
            acc = add_tile(tiles[0])
            for tile in tiles[1:]:
                acc = acc + add_tile(tile)
            part[at, :] = acc
            return carry

        lax.fori_loop(0, tok // ROWS, step, 0, unroll=2)
        return jnp.broadcast_to(jnp.sum(part[...], axis=1, keepdims=True) * (1.0 / width), (tok, LANES))

    def squares(at):
        middle = center[0, at, :]

        def body(tile):
            shifted = hidden[0, at, tile].astype(F32) - middle
            return shifted * shifted

        return body

    center[0] = row_sums(lambda at: lambda tile: hidden[0, at, tile].astype(F32))
    inv_std[0] = lax.rsqrt(row_sums(squares) + EPS)
    turn = frame % PAIR

    def adapt(i, carry):
        at = chunk_rows(i)
        middle, inv = center[0, at, :], inv_std[0, at, :]
        for tile in tiles:
            normed = by_sublane((hidden[0, at, tile].astype(F32) - middle) * inv)
            shaped = normed * scale8[:, tile] + shift8[:, tile]
            adapted[turn, at, tile] = shaped.reshape(ROWS, LANES).astype(BF16)
        return carry

    lax.fori_loop(0, tok // ROWS, adapt, 0, unroll=2)

    @pl.when(turn == PAIR - 1)
    def _():
        out = dot(weight[...], adapted[...].reshape(PAIR * tok, width), ((1,), (1,))).astype(BF16)
        grouped = dot(rows[...], out).astype(BF16)
        wide = []
        for j in range(PAIR * tok // LANES):
            tile = grouped[:, j * LANES : (j + 1) * LANES]
            wide.append(jnp.concatenate([tile[s * C : (s + 1) * C] for s in range(PATCH)], axis=1))
        pixels = dot(jnp.concatenate(wide, axis=0), perm[...]).astype(BF16)
        pixel_block = mine.shape[3]
        per_tile = PATCH * LANES // pixel_block
        for p in range(PAIR):
            f = frame - (PAIR - 1) + p
            target = f % n_eval
            place = f // n_eval
            for b in range(n_blk):
                row = (p * (tok // LANES) + b // per_tile) * C
                col = b % per_tile * pixel_block
                mine[f, b] = pixels[row : row + C, col : col + pixel_block]
            for b in range(n_blk):
                owner = e * n_blk + b
                own = (owner == t) & (target == e)
                dst = latent.at[target, place, t]

                @pl.when(own)
                def _():
                    pltpu.make_async_copy(mine.at[f, b], dst, out_recv.at[place, t]).start()

                @pl.when(jnp.logical_not(own))
                def _():
                    remote(mine.at[f, b], dst, out_send.at[f, b], out_recv.at[place, t], (owner, target)).start()

    def x_copy(r, d):
        there = 2 * ((x + d) % n_x) + core
        return remote(latent.at[e, r], latent.at[e, r], x_send.at[r, d - 1], x_recv.at[r, d - 1], (t, there))

    def core_copy(r, d):
        held = 2 * ((x + n_x - d) % n_x) + core
        return remote(latent.at[held, r], latent.at[held, r], c_send.at[r, d], c_recv.at[r, d], (t, partner))

    def first(r):
        for source in range(n_tm):
            pltpu.make_async_copy(mine.at[0, 0], latent.at[e, r, source], out_recv.at[r, source]).wait()
        for d in range(1, n_x):
            x_copy(r, d).start()
        core_copy(r, 0).start()

    def second(r):
        for d in range(1, n_x):
            x_copy(r, d).wait_recv()
            core_copy(r, d).start()

    for r in range(per):
        pl.when(frame == min((r + 2) * n_eval - 1, last))(functools.partial(first, r))
    for r in range(per):
        pl.when(frame == min((r + 3) * n_eval - 1, last))(functools.partial(second, r))

    @pl.when(frame == frames - 1)
    def _():
        for f in range(fd):
            for b in range(n_blk):
                owner = e * n_blk + b
                own = (owner == t) & (f % n_eval == e)
                when_not(
                    own,
                    lambda: remote(
                        mine.at[f, b], mine.at[f, b], out_send.at[f, b], out_recv.at[0, 0], (owner, f % n_eval)
                    ).wait_send(),
                )
        for r in range(per):
            for d in range(1, n_x):
                x_copy(r, d).wait_send()
            for d in range(n_x):
                core_copy(r, d).wait()
        row = lax.broadcasted_iota(jnp.int32, (n_win, LANES), 0)
        found = jnp.zeros((n_win, LANES), F32)
        for w in range(n_win):
            start = starts[w]

            def add(k, acc):
                g = start + k
                inner = g % fd
                block = latent[inner % n_eval, inner // n_eval, g // fd].astype(F32)
                return acc + jnp.abs(block - real[w, k].astype(F32))

            acc = lax.fori_loop(0, WIN, add, jnp.zeros(real.shape[2:], F32), unroll=3)
            total = jnp.sum(jnp.sum(acc, axis=0, keepdims=True), axis=1, keepdims=True)
            found = jnp.where(row == w, total, found)
        sums[t] = found
        for d in range(1, n_tm):
            there = (t + d) % n_tm
            remote(sums.at[t], sums.at[t], s_send.at[d - 1], s_recv.at[d - 1], (there, e)).start()
        for d in range(1, n_tm):
            origin = (t + n_tm - d) % n_tm
            remote(sums.at[origin], sums.at[origin], s_send.at[d - 1], s_recv.at[d - 1], (origin, e)).wait()
        result = sums[0]
        for other in range(1, n_tm):
            result = result + sums[other]
        totals[...] = result


def reduce_kernel(
    n_tm, n_eval, n_blk, starts, times, totals, real, fake, hidden, modulation, weight, center, inv_std,
    ups, mean_b, head_out, mod_out,
    grad, gain, from_core, half, from_x, rounded, landed, c_send, c_recv, x_send, x_recv, o_send, o_recv,
    adapted, d_adapted, shift8, scale8, perm, rows, head, sum_b, part, head_tiles, mod_part, *sum_scratch,
):
    step = pl.program_id(0)
    t = lax.axis_index("tm")
    e = lax.axis_index("eval")
    n_x = n_eval // 2
    x, core = e // 2, e % 2
    partner = 2 * x + 1 - core
    fd = grad.shape[0]
    owners = n_tm // n_eval
    mid = n_tm // 2
    home = t // n_blk
    slot = t % n_blk
    pixel_block = grad.shape[3]
    n_win = real.shape[0]
    tok, width = hidden.shape[1], hidden.shape[2]

    @pl.when(step == 0)
    def _():
        group = t // owners
        reducer = 2 * (group % n_x) + group // n_x
        for other in range(n_eval):
            when_not(other == e, lambda: greet((t, other)))
        for other in range(n_tm):
            when_not(other == t, lambda: greet((other, e)))
        for b in range(n_blk):
            when_not((e * n_blk + b == t) & (reducer == e), lambda: greet((e * n_blk + b, reducer)))
        own = jnp.where((home == e) & (reducer == e), 1, 0)
        pl.semaphore_wait(pltpu.get_barrier_semaphore(), n_eval - 1 + n_tm - 1 + owners - own)
        spread = totals[...] / float(WIN * C * pixel_block * n_tm) + 1e-05
        for w in range(n_win):
            level = times[w].astype(F32) / 1000.0
            gain[w] = jnp.broadcast_to(level / spread[w : w + 1, :], (SUB, LANES))
        head[...] = jnp.zeros_like(head)
        perm[...] = pixel_permutation(True)
        rows[...] = row_permutation(True)

    def core_copy(j):
        return remote(
            grad.at[j, pl.ds((1 - core) * mid, mid)], from_core.at[j], c_send.at[j], c_recv.at[j], (t, partner)
        )

    def x_copy(j, d):
        there = (x + d) % n_x
        return remote(
            half.at[j, pl.ds(there * owners, owners)], from_x.at[j, d - 1], x_send.at[j, d - 1], x_recv.at[j, d - 1],
            (t, 2 * there + core),
        )

    def owner_of(r):
        return (core * n_x + x) * owners + r

    def out_copy(j, r):
        return remote(
            rounded.at[j, r], landed.at[j, slot], o_send.at[j, r], o_recv.at[j, slot], (owner_of(r), home)
        )

    @pl.when(step < fd)
    def _():
        def build(o, carry):
            total = jnp.zeros((C, pixel_block), F32)
            for w in range(n_win):
                k = o * fd + step - starts[w]
                inside = jnp.where((k >= 0) & (k < WIN), 1.0, 0.0)
                k = jnp.clip(k, 0, WIN - 1)
                factor = gain[w] * inside
                factor = jnp.concatenate([factor] * (pixel_block // LANES), axis=1)
                factor = jnp.concatenate([factor] * (C // SUB), axis=0)
                total = total + factor * (fake[w, k].astype(F32) - real[w, k].astype(F32))
            grad[step, o] = total
            return carry

        lax.fori_loop(0, n_tm, build, 0)
        core_copy(step).start()

    @pl.when((step >= 1) & (step < fd + 1))
    def _():
        j = step - 1
        core_copy(j).wait_recv()
        half[j] = grad[j, pl.ds(core * mid, mid)] + from_core[j]
        for d in range(1, n_x):
            x_copy(j, d).start()

    @pl.when((step >= LAG - 2) & (step < fd + LAG - 2))
    def _():
        j = step - (LAG - 2)
        total = half[j, pl.ds(x * owners, owners)]
        for d in range(1, n_x):
            x_copy(j, d).wait_recv()
            total = total + from_x[j, d - 1]
        rounded[j] = total.astype(BF16)
        for r in range(owners):
            own = (owner_of(r) == t) & (home == e)

            @pl.when(own)
            def _():
                pltpu.make_async_copy(rounded.at[j, r], landed.at[j, slot], o_recv.at[j, slot]).start()

            @pl.when(jnp.logical_not(own))
            def _():
                out_copy(j, r).start()

    @pl.when(step >= LAG)
    def _():
        frame = step - LAG
        for b in range(n_blk):
            pltpu.make_async_copy(rounded.at[0, 0], landed.at[frame, b], o_recv.at[frame, b]).wait()
        size = LANES * PATCH
        flat = jnp.concatenate([landed[frame, b] for b in range(n_blk)], axis=1)
        wide = jnp.concatenate([flat[:, j * size : (j + 1) * size] for j in range(tok // LANES)], axis=0)
        wide = dot(wide, perm[...]).astype(BF16)
        blocks = []
        for j in range(tok // LANES):
            block = wide[j * C : (j + 1) * C]
            blocks.append(jnp.concatenate([block[:, s * LANES : (s + 1) * LANES] for s in range(PATCH)], axis=0))
        up = dot(rows[...], jnp.concatenate(blocks, axis=1)).astype(BF16)
        ups[0] = up
        shift8[...] = jnp.broadcast_to(modulation[0, 0:1, :], shift8.shape)
        scale8[...] = jnp.broadcast_to(1.0 + modulation[0, 1:2, :], scale8.shape)
        d_adapted[...] = dot(up, weight[...], ((0,), (0,)))
        up_sum = jnp.sum(up.astype(F32), axis=1, keepdims=True)
        per = fd // n_eval
        mod_part[frame // per, frame % per, 0:1, :] = jnp.sum(weight[...].astype(F32) * up_sum, axis=0, keepdims=True)
        sum_b[...] = jnp.zeros_like(sum_b)
        tiles = [slice(i * LANES, (i + 1) * LANES) for i in range(width // LANES)]

        def gather(i, carry):
            at = chunk_rows(i)
            middle, inv = center[0, at, :], inv_std[0, at, :]
            acc = jnp.zeros((ROWS // SUB, SUB, LANES), F32)
            for tile in tiles:
                normed = by_sublane((hidden[0, at, tile].astype(F32) - middle) * inv)
                scaled = normed * scale8[:, tile]
                adapted[at, tile] = (scaled + shift8[:, tile]).reshape(ROWS, LANES).astype(BF16)
                da = by_sublane(d_adapted[at, tile])
                acc = acc + da * scaled
                sum_b[:, tile] += jnp.sum(da * normed, axis=0)
            part[at, :] = acc.reshape(ROWS, LANES)
            return carry

        lax.fori_loop(0, tok // ROWS, gather, 0, unroll=2)
        mean_cross = jnp.sum(part[...], axis=1, keepdims=True) * (1.0 / width)
        mean_b[0] = mean_cross * inv_std[0] * inv_std[0]
        head[...] += dot(up, adapted[...])
        mod_part[frame // per, frame % per, 1:2, :] = jnp.sum(sum_b[...], axis=0, keepdims=True)

    @pl.when(step == pl.num_programs(0) - 1)
    def _():
        per = head_tiles.shape[2]
        place = 0
        for col in range(0, width, LANES):
            for r in range(0, head.shape[0], SUB):
                head_tiles[place // (per * n_tm), place // per % n_tm, place % per] = head[r : r + SUB, col : col + LANES]
                place += 1
        for place in range(place, n_eval * n_tm * per):
            head_tiles[place // (per * n_tm), place // per % n_tm, place % per] = jnp.zeros((SUB, LANES), F32)
        sum_parts(n_tm, n_eval, head_tiles, mod_part, head_out, mod_out, *sum_scratch)

        def drain(j, carry):
            core_copy(j).wait_send()
            for d in range(1, n_x):
                x_copy(j, d).wait_send()
            for r in range(owners):
                when_not((owner_of(r) == t) & (home == e), lambda: out_copy(j, r).wait_send())
            return carry

        lax.fori_loop(0, fd, drain, 0)


def backward_kernel(
    hidden, modulation, weight, center, inv_std, ups, mean_b, d_hidden, d_adapted, scale8, mean_a
):
    tok, width = hidden.shape[1], hidden.shape[2]
    scale = 1.0 + modulation[0, 1:2, :]
    scale8[...] = jnp.broadcast_to(scale, scale8.shape)
    up = ups[0]
    d_adapted[...] = dot(up, weight[...], ((0,), (0,)))

    level = jnp.sum(weight[...].astype(F32) * scale, axis=1, keepdims=True) * (1.0 / width)
    rest = jnp.broadcast_to(level, (level.shape[0], LANES))
    total = jnp.zeros((tok, LANES), F32)
    for _ in range(3):
        term = rest.astype(BF16)
        total = total + dot(up, term, ((0,), (0,)))
        rest = rest - term.astype(F32)
    mean_a[...] = total * inv_std[0]
    tiles = [slice(i * LANES, (i + 1) * LANES) for i in range(width // LANES)]

    def finish(i, carry):
        at = chunk_rows(i)
        middle, inv, first, second = center[0, at, :], inv_std[0, at, :], mean_a[at, :], mean_b[0, at, :]
        for tile in tiles:
            shifted = hidden[0, at, tile].astype(F32) - middle
            dn = (by_sublane(d_adapted[at, tile]) * scale8[:, tile]).reshape(ROWS, LANES) * inv
            d_hidden[0, at, tile] = (dn - first - shifted * second).astype(BF16)
        return carry

    lax.fori_loop(0, tok // ROWS, finish, 0, unroll=2)


def sum_parts(
    n_tm, n_eval, head, mod, head_out, mod_out,
    from_eval, from_tm, mod_in, a_send, a_recv, b_send, b_recv, g_send, g_recv, h_send, h_recv, m_send, m_recv,
    k_send, k_recv, head_all, mod_all, mine,
):
    t = lax.axis_index("tm")
    e = lax.axis_index("eval")
    def eval_peer(d):
        return (e + d) % n_eval

    def tm_peer(d):
        return (t + d) % n_tm

    def head_in(d):
        return remote(head.at[eval_peer(d)], from_eval.at[d - 1], a_send.at[d - 1], a_recv.at[d - 1], (t, eval_peer(d)))

    def mod_scatter(d):
        return remote(mod.at[eval_peer(d)], mod_in.at[d - 1], m_send.at[d - 1], m_recv.at[d - 1], (t, eval_peer(d)))

    for d in range(1, n_eval):
        head_in(d).start()
    for d in range(1, n_eval):
        mod_scatter(d).start()
    part = head[e]
    for d in range(1, n_eval):
        head_in(d).wait_recv()
        part = part + from_eval[d - 1]
    mine[...] = part

    def tm_in(d):
        return remote(mine.at[tm_peer(d)], from_tm.at[d - 1], b_send.at[d - 1], b_recv.at[d - 1], (tm_peer(d), e))

    for d in range(1, n_tm):
        tm_in(d).start()
    mod_sum = mod[e]
    for d in range(1, n_eval):
        mod_scatter(d).wait_recv()
        mod_sum = mod_sum + mod_in[d - 1]
    mod_all[e] = mod_sum

    def mod_spread(d):
        return remote(mod_all.at[e], mod_all.at[e], k_send.at[d - 1], k_recv.at[d - 1], (t, eval_peer(d)))

    for d in range(1, n_eval):
        mod_spread(d).start()
    total = mine[t]
    for d in range(1, n_tm):
        tm_in(d).wait_recv()
        total = total + from_tm[d - 1]
    head_all[e, t] = total

    def tm_spread(d):
        return remote(head_all.at[e, t], head_all.at[e, t], g_send.at[d - 1], g_recv.at[d - 1], (tm_peer(d), e))

    def eval_spread(d):
        return remote(head_all.at[e], head_all.at[e], h_send.at[d - 1], h_recv.at[d - 1], (t, eval_peer(d)))

    for d in range(1, n_tm):
        tm_spread(d).start()
    for d in range(1, n_tm):
        tm_spread(d).wait()
    for d in range(1, n_eval):
        eval_spread(d).start()
    for d in range(1, n_eval):
        head_in(d).wait_send()
        mod_scatter(d).wait_send()
        mod_spread(d).wait()
    for d in range(1, n_tm):
        tm_in(d).wait_send()
    mod_out[...] = mod_all[...]
    for d in range(1, n_eval):
        eval_spread(d).wait()
    per = head_all.shape[2]
    place = 0
    for col in range(0, head_out.shape[1], LANES):
        for r in range(0, head_out.shape[0], 8):
            head_out[r : r + 8, col : col + LANES] = head_all[place // (per * n_tm), place // per % n_tm, place % per]
            place += 1


def params(collective=None):
    if collective is None:
        return pltpu.CompilerParams(vmem_limit_bytes=VMEM_LIMIT)
    return pltpu.CompilerParams(vmem_limit_bytes=VMEM_LIMIT, collective_id=collective, has_side_effects=True)


def per_device(hidden, modulation, head_weight, real_score, fake_score, window_start, timestep):
    fd, tok, width = hidden.shape
    n_tm = lax.axis_size("tm")
    n_eval = lax.axis_size("eval")
    n_win = real_score.shape[0]
    pixel_block = real_score.shape[3]
    n_blk = tok * PATCH // pixel_block
    per = fd // n_eval
    n_x = n_eval // 2
    size = LANES * PATCH
    dma = pltpu.SemaphoreType.DMA
    vmem = pl.BlockSpec(memory_space=pltpu.VMEM)
    smem = pl.BlockSpec(memory_space=pltpu.SMEM)
    by_frame = pl.BlockSpec((1, tok, width), lambda f: (f, 0, 0))
    mod_frame = pl.BlockSpec((1, 2, width), lambda f: (f, 0, 0))
    stat_frame = pl.BlockSpec((1, tok, LANES), lambda f: (f, 0, 0))
    extra_x = max(n_x - 1, 1)

    totals, center, inv_std = pl.pallas_call(
        functools.partial(forward_kernel, n_tm, n_eval, n_blk),
        grid=(fd,),
        out_shape=(
            jax.ShapeDtypeStruct((n_win, LANES), F32),
            jax.ShapeDtypeStruct((fd, tok, LANES), F32),
            jax.ShapeDtypeStruct((fd, tok, LANES), F32),
        ),
        in_specs=[smem, by_frame, mod_frame, vmem, vmem],
        out_specs=(pl.BlockSpec((n_win, LANES), lambda f: (0, 0)), stat_frame, stat_frame),
        scratch_shapes=[
            pltpu.VMEM((PAIR, tok, width), BF16),
            pltpu.VMEM((tok, LANES), F32),
            pltpu.VMEM((SUB, width), F32),
            pltpu.VMEM((SUB, width), F32),
            pltpu.VMEM((size, size), BF16),
            pltpu.VMEM((C * PATCH, C * PATCH), BF16),
            pltpu.VMEM((fd, n_blk, C, pixel_block), BF16),
            pltpu.VMEM((n_eval, per, n_tm, C, pixel_block), BF16),
            pltpu.VMEM((n_tm, n_win, LANES), F32),
            dma((fd, n_blk)),
            dma((per, n_tm)),
            dma((per, extra_x)),
            dma((per, extra_x)),
            dma((per, n_x)),
            dma((per, n_x)),
            dma((n_tm - 1,)),
            dma((n_tm - 1,)),
        ],
        compiler_params=params(0),
        name="forward",
    )(window_start, hidden, modulation, head_weight, real_score)

    head_tiles = width // LANES * (C * PATCH // SUB)
    head_shape = (n_eval, n_tm, pl.cdiv(head_tiles, n_eval * n_tm), SUB, LANES)
    mod_shape = (n_eval, per, 2, width)
    owners = n_tm // n_eval
    e_sem, t_sem = dma((n_eval - 1,)), dma((n_tm - 1,))

    def late(*shape):
        return pl.BlockSpec((1,) + shape, lambda i: (jnp.maximum(i - LAG, 0),) + (0,) * len(shape))

    def whole(shape):
        return pl.BlockSpec(shape, lambda i: (0,) * len(shape))

    ups, mean_b, head_grad, mod_grad = pl.pallas_call(
        functools.partial(reduce_kernel, n_tm, n_eval, n_blk),
        grid=(fd + LAG,),
        out_shape=(
            jax.ShapeDtypeStruct((fd, C * PATCH, tok), BF16),
            jax.ShapeDtypeStruct((fd, tok, LANES), F32),
            jax.ShapeDtypeStruct(head_weight.shape, F32),
            jax.ShapeDtypeStruct(mod_shape, F32),
        ),
        in_specs=[
            smem, smem, vmem, vmem, vmem,
            late(tok, width), late(2, width), vmem, late(tok, LANES), late(tok, LANES),
        ],
        out_specs=(late(C * PATCH, tok), late(tok, LANES), whole(head_weight.shape), whole(mod_shape)),
        scratch_shapes=[
            pltpu.VMEM((fd, n_tm, C, pixel_block), F32),
            pltpu.VMEM((n_win, SUB, LANES), F32),
            pltpu.VMEM((fd, n_tm // 2, C, pixel_block), F32),
            pltpu.VMEM((fd, n_tm // 2, C, pixel_block), F32),
            pltpu.VMEM((fd, extra_x, owners, C, pixel_block), F32),
            pltpu.VMEM((fd, owners, C, pixel_block), BF16),
            pltpu.VMEM((fd, n_blk, C, pixel_block), BF16),
            dma((fd,)),
            dma((fd,)),
            dma((fd, extra_x)),
            dma((fd, extra_x)),
            dma((fd, owners)),
            dma((fd, n_blk)),
            pltpu.VMEM((tok, width), BF16),
            pltpu.VMEM((tok, width), F32),
            pltpu.VMEM((SUB, width), F32),
            pltpu.VMEM((SUB, width), F32),
            pltpu.VMEM((size, size), BF16),
            pltpu.VMEM((C * PATCH, C * PATCH), BF16),
            pltpu.VMEM((C * PATCH, width), F32),
            pltpu.VMEM((SUB, width), F32),
            pltpu.VMEM((tok, LANES), F32),
            pltpu.VMEM(head_shape, F32),
            pltpu.VMEM(mod_shape, F32),
            pltpu.VMEM((n_eval - 1,) + head_shape[1:], F32),
            pltpu.VMEM((n_tm - 1,) + head_shape[2:], F32),
            pltpu.VMEM((n_eval - 1,) + mod_shape[1:], F32),
            e_sem, e_sem, t_sem, t_sem, t_sem, t_sem, e_sem, e_sem, e_sem, e_sem, e_sem, e_sem,
            pltpu.VMEM(head_shape, F32),
            pltpu.VMEM(mod_shape, F32),
            pltpu.VMEM(head_shape[1:], F32),
        ],
        compiler_params=params(1),
        name="reduce",
    )(
        window_start, timestep, totals, real_score, fake_score,
        hidden, modulation, head_weight, center, inv_std,
    )

    d_hidden = pl.pallas_call(
        backward_kernel,
        grid=(fd,),
        out_shape=jax.ShapeDtypeStruct(hidden.shape, BF16),
        in_specs=[
            by_frame, mod_frame, vmem, stat_frame, stat_frame,
            pl.BlockSpec((1, C * PATCH, tok), lambda f: (f, 0, 0)), stat_frame,
        ],
        out_specs=by_frame,
        scratch_shapes=[
            pltpu.VMEM((tok, width), F32),
            pltpu.VMEM((SUB, width), F32),
            pltpu.VMEM((tok, LANES), F32),
        ],
        compiler_params=params(),
        name="backward",
    )(hidden, modulation, head_weight, center, inv_std, ups, mean_b)
    return (d_hidden, head_grad, mod_grad.reshape(modulation.shape))


def solution(mesh):
    placed = (
        P("tm", "eval", None),
        P("tm", None, None),
        P(),
        P("eval", None, None, "tm"),
        P("eval", None, None, "tm"),
        P("eval"),
        P("eval"),
    )
    return jax.shard_map(
        per_device,
        mesh=mesh,
        in_specs=placed,
        out_specs=(P("tm", "eval", None), P(), P("tm", None, None)),
        check_vma=False,
    )
```

```python
import functools

import jax
import jax.numpy as jnp
from jax import lax
from jax.experimental import pallas as pl
from jax.experimental.pallas import tpu as pltpu
from jax.sharding import PartitionSpec as P

C = 16
PATCH = 4
WIN = 21
TOK = 1024
EPS = 1e-06
LANES = 128
ROWS = 32
SUB = 8
PAIR = 2
LAG = 5
MESH = pl.DeviceIdType.MESH
VMEM_LIMIT = 56 * 1024 * 1024
F32 = jnp.float32
BF16 = jnp.bfloat16


def remote(src, dst, send_sem, recv_sem, device):
    return pltpu.make_async_remote_copy(
        src_ref=src, dst_ref=dst, send_sem=send_sem, recv_sem=recv_sem, device_id=device, device_id_type=MESH
    )


def greet(device):
    pl.semaphore_signal(pltpu.get_barrier_semaphore(), inc=1, device_id=device, device_id_type=MESH)


def when_not(flag, action):
    pl.when(jnp.logical_not(flag))(action)


def pixel_permutation(inverse):
    size = PATCH * LANES
    lane = lax.broadcasted_iota(jnp.int32, (size, size), 1 if inverse else 0)
    pixel = lax.broadcasted_iota(jnp.int32, (size, size), 0 if inverse else 1)
    return jnp.where(pixel == (lane & (LANES - 1)) * PATCH + (lane >> 7), 1.0, 0.0).astype(BF16)


def row_permutation(inverse):
    size = C * PATCH
    grouped = lax.broadcasted_iota(jnp.int32, (size, size), 1 if inverse else 0)
    mixed = lax.broadcasted_iota(jnp.int32, (size, size), 0 if inverse else 1)
    return jnp.where(mixed == (grouped & (C - 1)) * PATCH + (grouped >> 4), 1.0, 0.0).astype(BF16)


def chunk_rows(i):
    return pl.ds(pl.multiple_of(i * ROWS, ROWS), ROWS)


def by_sublane(block):
    return block.reshape(block.shape[0] // SUB, SUB, block.shape[1])


def dot(a, b, dims=((1,), (0,))):
    return lax.dot_general(a, b, (dims, ((), ())), preferred_element_type=F32)


def forward_kernel(
    n_tm, n_eval, n_blk, starts, hidden, modulation, weight, real, totals, center, inv_std,
    adapted, part, ones, shift8, scale8, perm, rows, mine, latent, sums, out_send, out_recv, x_send, x_recv, c_send, c_recv, s_send, s_recv,
):
    frame = pl.program_id(0)
    frames = pl.num_programs(0)
    fd = mine.shape[0]
    last = fd - 1
    t = lax.axis_index("tm")
    e = lax.axis_index("eval")
    n_x = n_eval // 2
    x, core = e // 2, e % 2
    partner = 2 * x + 1 - core
    per = fd // n_eval
    tok, width = hidden.shape[1], hidden.shape[2]
    n_win = real.shape[0]

    @pl.when(frame == 0)
    def _():
        source = t // n_blk
        for other in range(n_tm):
            when_not((other == t) & (source == e), lambda: greet((other, source)))
            when_not(other == t, lambda: greet((other, e)))
        for other in range(n_eval):
            when_not(other == e, lambda: greet((t, other)))
        own = jnp.where(source == e, 1, 0)
        pl.semaphore_wait(pltpu.get_barrier_semaphore(), n_tm - own + n_tm - 1 + n_eval - 1)
        ones[...] = jnp.ones_like(ones)
        perm[...] = pixel_permutation(False)
        rows[...] = row_permutation(False)

    tiles = [slice(i * LANES, (i + 1) * LANES) for i in range(width // LANES)]
    shift8[...] = jnp.broadcast_to(modulation[0, 0:1, :], shift8.shape)
    scale8[...] = jnp.broadcast_to(1.0 + modulation[0, 1:2, :], scale8.shape)

    def row_sums(body):
        def step(i, carry):
            at = chunk_rows(i)
            add_tile = body(at)
            acc = add_tile(tiles[0])
            for tile in tiles[1:]:
                acc = acc + add_tile(tile)
            part[at, :] = acc
            return carry

        lax.fori_loop(0, tok // ROWS, step, 0, unroll=2)
        return jnp.broadcast_to(jnp.sum(part[...], axis=1, keepdims=True) * (1.0 / width), (tok, LANES))

    def squares(at):
        middle = center[0, at, :]

        def body(tile):
            shifted = hidden[0, at, tile].astype(F32) - middle
            return shifted * shifted

        return body

    center[0] = dot(hidden[0], ones[...]) * (1.0 / width)
    inv_std[0] = lax.rsqrt(row_sums(squares) + EPS)
    turn = frame % PAIR

    def adapt(i, carry):
        at = chunk_rows(i)
        middle, inv = center[0, at, :], inv_std[0, at, :]
        for tile in tiles:
            normed = by_sublane((hidden[0, at, tile].astype(F32) - middle) * inv)
            shaped = normed * scale8[:, tile] + shift8[:, tile]
            adapted[turn, at, tile] = shaped.reshape(ROWS, LANES).astype(BF16)
        return carry

    lax.fori_loop(0, tok // ROWS, adapt, 0, unroll=2)

    @pl.when(turn == PAIR - 1)
    def _():
        out = dot(weight[...], adapted[...].reshape(PAIR * tok, width), ((1,), (1,))).astype(BF16)
        grouped = dot(rows[...], out).astype(BF16)
        wide = []
        for j in range(PAIR * tok // LANES):
            tile = grouped[:, j * LANES : (j + 1) * LANES]
            wide.append(jnp.concatenate([tile[s * C : (s + 1) * C] for s in range(PATCH)], axis=1))
        pixels = dot(jnp.concatenate(wide, axis=0), perm[...]).astype(BF16)
        pixel_block = mine.shape[3]
        per_tile = PATCH * LANES // pixel_block
        for p in range(PAIR):
            f = frame - (PAIR - 1) + p
            target = f % n_eval
            place = f // n_eval
            for b in range(n_blk):
                row = (p * (tok // LANES) + b // per_tile) * C
                col = b % per_tile * pixel_block
                mine[f, b] = pixels[row : row + C, col : col + pixel_block]
            for b in range(n_blk):
                owner = e * n_blk + b
                own = (owner == t) & (target == e)
                dst = latent.at[target, place, t]

                @pl.when(own)
                def _():
                    pltpu.make_async_copy(mine.at[f, b], dst, out_recv.at[place, t]).start()

                @pl.when(jnp.logical_not(own))
                def _():
                    remote(mine.at[f, b], dst, out_send.at[f, b], out_recv.at[place, t], (owner, target)).start()

    def x_copy(r, d):
        there = 2 * ((x + d) % n_x) + core
        return remote(latent.at[e, r], latent.at[e, r], x_send.at[r, d - 1], x_recv.at[r, d - 1], (t, there))

    def core_copy(r, d):
        held = 2 * ((x + n_x - d) % n_x) + core
        return remote(latent.at[held, r], latent.at[held, r], c_send.at[r, d], c_recv.at[r, d], (t, partner))

    def first(r):
        for source in range(n_tm):
            pltpu.make_async_copy(mine.at[0, 0], latent.at[e, r, source], out_recv.at[r, source]).wait()
        for d in range(1, n_x):
            x_copy(r, d).start()
        core_copy(r, 0).start()

    def second(r):
        for d in range(1, n_x):
            x_copy(r, d).wait_recv()
            core_copy(r, d).start()

    for r in range(per):
        pl.when(frame == min((r + 2) * n_eval - 1, last))(functools.partial(first, r))
    for r in range(per):
        pl.when(frame == min((r + 3) * n_eval - 1, last))(functools.partial(second, r))

    @pl.when(frame == frames - 1)
    def _():
        for f in range(fd):
            for b in range(n_blk):
                owner = e * n_blk + b
                own = (owner == t) & (f % n_eval == e)
                when_not(
                    own,
                    lambda: remote(
                        mine.at[f, b], mine.at[f, b], out_send.at[f, b], out_recv.at[0, 0], (owner, f % n_eval)
                    ).wait_send(),
                )
        for r in range(per):
            for d in range(1, n_x):
                x_copy(r, d).wait_send()
            for d in range(n_x):
                core_copy(r, d).wait()
        row = lax.broadcasted_iota(jnp.int32, (n_win, LANES), 0)
        found = jnp.zeros((n_win, LANES), F32)
        for w in range(n_win):
            start = starts[w]

            def add(k, acc):
                g = start + k
                inner = g % fd
                block = latent[inner % n_eval, inner // n_eval, g // fd].astype(F32)
                return acc + jnp.abs(block - real[w, k].astype(F32))

            acc = lax.fori_loop(0, WIN, add, jnp.zeros(real.shape[2:], F32), unroll=3)
            total = jnp.sum(jnp.sum(acc, axis=0, keepdims=True), axis=1, keepdims=True)
            found = jnp.where(row == w, total, found)
        sums[t] = found
        for d in range(1, n_tm):
            there = (t + d) % n_tm
            remote(sums.at[t], sums.at[t], s_send.at[d - 1], s_recv.at[d - 1], (there, e)).start()
        for d in range(1, n_tm):
            origin = (t + n_tm - d) % n_tm
            remote(sums.at[origin], sums.at[origin], s_send.at[d - 1], s_recv.at[d - 1], (origin, e)).wait()
        result = sums[0]
        for other in range(1, n_tm):
            result = result + sums[other]
        totals[...] = result


def reduce_kernel(
    n_tm, n_eval, n_blk, starts, times, totals, real, fake, hidden, modulation, weight, center, inv_std,
    ups, mean_b, head_out, mod_out,
    grad, gain, from_core, half, from_x, rounded, landed, c_send, c_recv, x_send, x_recv, o_send, o_recv,
    adapted, d_adapted, shift8, scale8, perm, rows, head, sum_b, part, head_tiles, mod_part, *sum_scratch,
):
    step = pl.program_id(0)
    t = lax.axis_index("tm")
    e = lax.axis_index("eval")
    n_x = n_eval // 2
    x, core = e // 2, e % 2
    partner = 2 * x + 1 - core
    fd = grad.shape[0]
    owners = n_tm // n_eval
    mid = n_tm // 2
    home = t // n_blk
    slot = t % n_blk
    pixel_block = grad.shape[3]
    n_win = real.shape[0]
    tok, width = hidden.shape[1], hidden.shape[2]

    @pl.when(step == 0)
    def _():
        group = t // owners
        reducer = 2 * (group % n_x) + group // n_x
        for other in range(n_eval):
            when_not(other == e, lambda: greet((t, other)))
        for other in range(n_tm):
            when_not(other == t, lambda: greet((other, e)))
        for b in range(n_blk):
            when_not((e * n_blk + b == t) & (reducer == e), lambda: greet((e * n_blk + b, reducer)))
        own = jnp.where((home == e) & (reducer == e), 1, 0)
        pl.semaphore_wait(pltpu.get_barrier_semaphore(), n_eval - 1 + n_tm - 1 + owners - own)
        spread = totals[...] / float(WIN * C * pixel_block * n_tm) + 1e-05
        for w in range(n_win):
            level = times[w].astype(F32) / 1000.0
            gain[w] = jnp.broadcast_to(level / spread[w : w + 1, :], (SUB, LANES))
        head[...] = jnp.zeros_like(head)
        perm[...] = pixel_permutation(True)
        rows[...] = row_permutation(True)

    def core_copy(j):
        return remote(
            grad.at[j, pl.ds((1 - core) * mid, mid)], from_core.at[j], c_send.at[j], c_recv.at[j], (t, partner)
        )

    def x_copy(j, d):
        there = (x + d) % n_x
        return remote(
            half.at[j, pl.ds(there * owners, owners)], from_x.at[j, d - 1], x_send.at[j, d - 1], x_recv.at[j, d - 1],
            (t, 2 * there + core),
        )

    def owner_of(r):
        return (core * n_x + x) * owners + r

    def out_copy(j, r):
        return remote(
            rounded.at[j, r], landed.at[j, slot], o_send.at[j, r], o_recv.at[j, slot], (owner_of(r), home)
        )

    @pl.when(step < fd)
    def _():
        def build(o, carry):
            total = jnp.zeros((C, pixel_block), F32)
            for w in range(n_win):
                k = o * fd + step - starts[w]
                inside = jnp.where((k >= 0) & (k < WIN), 1.0, 0.0)
                k = jnp.clip(k, 0, WIN - 1)
                factor = gain[w] * inside
                factor = jnp.concatenate([factor] * (pixel_block // LANES), axis=1)
                factor = jnp.concatenate([factor] * (C // SUB), axis=0)
                total = total + factor * (fake[w, k].astype(F32) - real[w, k].astype(F32))
            grad[step, o] = total
            return carry

        lax.fori_loop(0, n_tm, build, 0)
        core_copy(step).start()

    @pl.when((step >= 1) & (step < fd + 1))
    def _():
        j = step - 1
        core_copy(j).wait_recv()
        half[j] = grad[j, pl.ds(core * mid, mid)] + from_core[j]
        for d in range(1, n_x):
            x_copy(j, d).start()

    @pl.when((step >= LAG - 2) & (step < fd + LAG - 2))
    def _():
        j = step - (LAG - 2)
        total = half[j, pl.ds(x * owners, owners)]
        for d in range(1, n_x):
            x_copy(j, d).wait_recv()
            total = total + from_x[j, d - 1]
        rounded[j] = total.astype(BF16)
        for r in range(owners):
            own = (owner_of(r) == t) & (home == e)

            @pl.when(own)
            def _():
                pltpu.make_async_copy(rounded.at[j, r], landed.at[j, slot], o_recv.at[j, slot]).start()

            @pl.when(jnp.logical_not(own))
            def _():
                out_copy(j, r).start()

    @pl.when(step >= LAG)
    def _():
        frame = step - LAG
        for b in range(n_blk):
            pltpu.make_async_copy(rounded.at[0, 0], landed.at[frame, b], o_recv.at[frame, b]).wait()
        size = LANES * PATCH
        flat = jnp.concatenate([landed[frame, b] for b in range(n_blk)], axis=1)
        wide = jnp.concatenate([flat[:, j * size : (j + 1) * size] for j in range(tok // LANES)], axis=0)
        wide = dot(wide, perm[...]).astype(BF16)
        blocks = []
        for j in range(tok // LANES):
            block = wide[j * C : (j + 1) * C]
            blocks.append(jnp.concatenate([block[:, s * LANES : (s + 1) * LANES] for s in range(PATCH)], axis=0))
        up = dot(rows[...], jnp.concatenate(blocks, axis=1)).astype(BF16)
        ups[0] = up
        shift8[...] = jnp.broadcast_to(modulation[0, 0:1, :], shift8.shape)
        scale8[...] = jnp.broadcast_to(1.0 + modulation[0, 1:2, :], scale8.shape)
        d_adapted[...] = dot(up, weight[...], ((0,), (0,)))
        up_sum = jnp.sum(up.astype(F32), axis=1, keepdims=True)
        per = fd // n_eval
        mod_part[frame // per, frame % per, 0:1, :] = jnp.sum(weight[...].astype(F32) * up_sum, axis=0, keepdims=True)
        sum_b[...] = jnp.zeros_like(sum_b)
        tiles = [slice(i * LANES, (i + 1) * LANES) for i in range(width // LANES)]

        def gather(i, carry):
            at = chunk_rows(i)
            middle, inv = center[0, at, :], inv_std[0, at, :]
            acc = jnp.zeros((ROWS // SUB, SUB, LANES), F32)
            for tile in tiles:
                normed = by_sublane((hidden[0, at, tile].astype(F32) - middle) * inv)
                scaled = normed * scale8[:, tile]
                adapted[at, tile] = (scaled + shift8[:, tile]).reshape(ROWS, LANES).astype(BF16)
                da = by_sublane(d_adapted[at, tile])
                acc = acc + da * scaled
                sum_b[:, tile] += jnp.sum(da * normed, axis=0)
            part[at, :] = acc.reshape(ROWS, LANES)
            return carry

        lax.fori_loop(0, tok // ROWS, gather, 0, unroll=2)
        mean_cross = jnp.sum(part[...], axis=1, keepdims=True) * (1.0 / width)
        mean_b[0] = mean_cross * inv_std[0] * inv_std[0]
        head[...] += dot(up, adapted[...])
        mod_part[frame // per, frame % per, 1:2, :] = jnp.sum(sum_b[...], axis=0, keepdims=True)
        mod_in, m_send, m_recv = sum_scratch[2], sum_scratch[11], sum_scratch[12]
        for d in range(1, n_eval):
            peer = (e + d) % n_eval
            piece = remote(mod_part.at[peer], mod_in.at[d - 1], m_send.at[d - 1], m_recv.at[d - 1], (t, peer))
            pl.when(frame == (peer + 1) * per - 1)(lambda: piece.start())

    @pl.when(step == pl.num_programs(0) - 1)
    def _():
        per = head_tiles.shape[2]
        place = 0
        for col in range(0, width, LANES):
            for r in range(0, head.shape[0], SUB):
                head_tiles[place // (per * n_tm), place // per % n_tm, place % per] = head[r : r + SUB, col : col + LANES]
                place += 1
        for place in range(place, n_eval * n_tm * per):
            head_tiles[place // (per * n_tm), place // per % n_tm, place % per] = jnp.zeros((SUB, LANES), F32)
        sum_parts(n_tm, n_eval, head_tiles, mod_part, head_out, mod_out, *sum_scratch)

        def drain(j, carry):
            core_copy(j).wait_send()
            for d in range(1, n_x):
                x_copy(j, d).wait_send()
            for r in range(owners):
                when_not((owner_of(r) == t) & (home == e), lambda: out_copy(j, r).wait_send())
            return carry

        lax.fori_loop(0, fd, drain, 0)


def backward_kernel(
    hidden, modulation, weight, center, inv_std, ups, mean_b, d_hidden, d_adapted, scale8, mean_a
):
    tok, width = hidden.shape[1], hidden.shape[2]
    scale = 1.0 + modulation[0, 1:2, :]
    scale8[...] = jnp.broadcast_to(scale, scale8.shape)
    up = ups[0]
    d_adapted[...] = dot(up, weight[...], ((0,), (0,)))

    level = jnp.sum(weight[...].astype(F32) * scale, axis=1, keepdims=True) * (1.0 / width)
    rest = jnp.broadcast_to(level, (level.shape[0], LANES))
    terms = []
    for _ in range(3):
        terms.append(rest.astype(BF16))
        rest = rest - terms[-1].astype(F32)
    total = dot(jnp.concatenate([up] * 3, axis=0), jnp.concatenate(terms, axis=0), ((0,), (0,)))
    mean_a[...] = total * inv_std[0]
    tiles = [slice(i * LANES, (i + 1) * LANES) for i in range(width // LANES)]

    def finish(i, carry):
        at = chunk_rows(i)
        middle, inv, first, second = center[0, at, :], inv_std[0, at, :], mean_a[at, :], mean_b[0, at, :]
        for tile in tiles:
            shifted = hidden[0, at, tile].astype(F32) - middle
            dn = (by_sublane(d_adapted[at, tile]) * scale8[:, tile]).reshape(ROWS, LANES) * inv
            d_hidden[0, at, tile] = (dn - first - shifted * second).astype(BF16)
        return carry

    lax.fori_loop(0, tok // ROWS, finish, 0, unroll=2)


def sum_parts(
    n_tm, n_eval, head, mod, head_out, mod_out,
    from_eval, from_tm, mod_in, a_send, a_recv, b_send, b_recv, g_send, g_recv, h_send, h_recv, m_send, m_recv,
    k_send, k_recv, head_all, mod_all, mine,
):
    t = lax.axis_index("tm")
    e = lax.axis_index("eval")
    def eval_peer(d):
        return (e + d) % n_eval

    def tm_peer(d):
        return (t + d) % n_tm

    def head_in(d):
        return remote(head.at[eval_peer(d)], from_eval.at[d - 1], a_send.at[d - 1], a_recv.at[d - 1], (t, eval_peer(d)))

    def mod_scatter(d):
        return remote(mod.at[eval_peer(d)], mod_in.at[d - 1], m_send.at[d - 1], m_recv.at[d - 1], (t, eval_peer(d)))

    for d in range(1, n_eval):
        head_in(d).start()
    part = head[e]
    for d in range(1, n_eval):
        head_in(d).wait_recv()
        part = part + from_eval[d - 1]
    mine[...] = part

    def tm_in(d):
        return remote(mine.at[tm_peer(d)], from_tm.at[d - 1], b_send.at[d - 1], b_recv.at[d - 1], (tm_peer(d), e))

    for d in range(1, n_tm):
        tm_in(d).start()
    mod_sum = mod[e]
    for d in range(1, n_eval):
        mod_scatter(d).wait_recv()
        mod_sum = mod_sum + mod_in[d - 1]
    mod_all[e] = mod_sum

    def mod_spread(d):
        return remote(mod_all.at[e], mod_all.at[e], k_send.at[d - 1], k_recv.at[d - 1], (t, eval_peer(d)))

    for d in range(1, n_eval):
        mod_spread(d).start()
    total = mine[t]
    for d in range(1, n_tm):
        tm_in(d).wait_recv()
        total = total + from_tm[d - 1]
    head_all[e, t] = total

    def tm_spread(d):
        return remote(head_all.at[e, t], head_all.at[e, t], g_send.at[d - 1], g_recv.at[d - 1], (tm_peer(d), e))

    def eval_spread(d):
        return remote(head_all.at[e], head_all.at[e], h_send.at[d - 1], h_recv.at[d - 1], (t, eval_peer(d)))

    for d in range(1, n_tm):
        tm_spread(d).start()
    for d in range(1, n_tm):
        tm_spread(d).wait()
    for d in range(1, n_eval):
        eval_spread(d).start()
    for d in range(1, n_eval):
        head_in(d).wait_send()
        mod_scatter(d).wait_send()
        mod_spread(d).wait()
    for d in range(1, n_tm):
        tm_in(d).wait_send()
    mod_out[...] = mod_all[...]
    for d in range(1, n_eval):
        eval_spread(d).wait()
    per = head_all.shape[2]
    place = 0
    for col in range(0, head_out.shape[1], LANES):
        for r in range(0, head_out.shape[0], 8):
            head_out[r : r + 8, col : col + LANES] = head_all[place // (per * n_tm), place // per % n_tm, place % per]
            place += 1


def params(collective=None):
    if collective is None:
        return pltpu.CompilerParams(vmem_limit_bytes=VMEM_LIMIT)
    return pltpu.CompilerParams(vmem_limit_bytes=VMEM_LIMIT, collective_id=collective, has_side_effects=True)


def per_device(hidden, modulation, head_weight, real_score, fake_score, window_start, timestep):
    fd, tok, width = hidden.shape
    n_tm = lax.axis_size("tm")
    n_eval = lax.axis_size("eval")
    n_win = real_score.shape[0]
    pixel_block = real_score.shape[3]
    n_blk = tok * PATCH // pixel_block
    per = fd // n_eval
    n_x = n_eval // 2
    size = LANES * PATCH
    dma = pltpu.SemaphoreType.DMA
    vmem = pl.BlockSpec(memory_space=pltpu.VMEM)
    smem = pl.BlockSpec(memory_space=pltpu.SMEM)
    by_frame = pl.BlockSpec((1, tok, width), lambda f: (f, 0, 0))
    mod_frame = pl.BlockSpec((1, 2, width), lambda f: (f, 0, 0))
    stat_frame = pl.BlockSpec((1, tok, LANES), lambda f: (f, 0, 0))
    extra_x = max(n_x - 1, 1)

    totals, center, inv_std = pl.pallas_call(
        functools.partial(forward_kernel, n_tm, n_eval, n_blk),
        grid=(fd,),
        out_shape=(
            jax.ShapeDtypeStruct((n_win, LANES), F32),
            jax.ShapeDtypeStruct((fd, tok, LANES), F32),
            jax.ShapeDtypeStruct((fd, tok, LANES), F32),
        ),
        in_specs=[smem, by_frame, mod_frame, vmem, vmem],
        out_specs=(pl.BlockSpec((n_win, LANES), lambda f: (0, 0)), stat_frame, stat_frame),
        scratch_shapes=[
            pltpu.VMEM((PAIR, tok, width), BF16),
            pltpu.VMEM((tok, LANES), F32),
            pltpu.VMEM((width, LANES), BF16),
            pltpu.VMEM((SUB, width), F32),
            pltpu.VMEM((SUB, width), F32),
            pltpu.VMEM((size, size), BF16),
            pltpu.VMEM((C * PATCH, C * PATCH), BF16),
            pltpu.VMEM((fd, n_blk, C, pixel_block), BF16),
            pltpu.VMEM((n_eval, per, n_tm, C, pixel_block), BF16),
            pltpu.VMEM((n_tm, n_win, LANES), F32),
            dma((fd, n_blk)),
            dma((per, n_tm)),
            dma((per, extra_x)),
            dma((per, extra_x)),
            dma((per, n_x)),
            dma((per, n_x)),
            dma((n_tm - 1,)),
            dma((n_tm - 1,)),
        ],
        compiler_params=params(0),
        name="forward",
    )(window_start, hidden, modulation, head_weight, real_score)

    head_tiles = width // LANES * (C * PATCH // SUB)
    head_shape = (n_eval, n_tm, pl.cdiv(head_tiles, n_eval * n_tm), SUB, LANES)
    mod_shape = (n_eval, per, 2, width)
    owners = n_tm // n_eval
    e_sem, t_sem = dma((n_eval - 1,)), dma((n_tm - 1,))

    def late(*shape):
        return pl.BlockSpec((1,) + shape, lambda i: (jnp.maximum(i - LAG, 0),) + (0,) * len(shape))

    def whole(shape):
        return pl.BlockSpec(shape, lambda i: (0,) * len(shape))

    ups, mean_b, head_grad, mod_grad = pl.pallas_call(
        functools.partial(reduce_kernel, n_tm, n_eval, n_blk),
        grid=(fd + LAG,),
        out_shape=(
            jax.ShapeDtypeStruct((fd, C * PATCH, tok), BF16),
            jax.ShapeDtypeStruct((fd, tok, LANES), F32),
            jax.ShapeDtypeStruct(head_weight.shape, F32),
            jax.ShapeDtypeStruct(mod_shape, F32),
        ),
        in_specs=[
            smem, smem, vmem, vmem, vmem,
            late(tok, width), late(2, width), vmem, late(tok, LANES), late(tok, LANES),
        ],
        out_specs=(late(C * PATCH, tok), late(tok, LANES), whole(head_weight.shape), whole(mod_shape)),
        scratch_shapes=[
            pltpu.VMEM((fd, n_tm, C, pixel_block), F32),
            pltpu.VMEM((n_win, SUB, LANES), F32),
            pltpu.VMEM((fd, n_tm // 2, C, pixel_block), F32),
            pltpu.VMEM((fd, n_tm // 2, C, pixel_block), F32),
            pltpu.VMEM((fd, extra_x, owners, C, pixel_block), F32),
            pltpu.VMEM((fd, owners, C, pixel_block), BF16),
            pltpu.VMEM((fd, n_blk, C, pixel_block), BF16),
            dma((fd,)),
            dma((fd,)),
            dma((fd, extra_x)),
            dma((fd, extra_x)),
            dma((fd, owners)),
            dma((fd, n_blk)),
            pltpu.VMEM((tok, width), BF16),
            pltpu.VMEM((tok, width), F32),
            pltpu.VMEM((SUB, width), F32),
            pltpu.VMEM((SUB, width), F32),
            pltpu.VMEM((size, size), BF16),
            pltpu.VMEM((C * PATCH, C * PATCH), BF16),
            pltpu.VMEM((C * PATCH, width), F32),
            pltpu.VMEM((SUB, width), F32),
            pltpu.VMEM((tok, LANES), F32),
            pltpu.VMEM(head_shape, F32),
            pltpu.VMEM(mod_shape, F32),
            pltpu.VMEM((n_eval - 1,) + head_shape[1:], F32),
            pltpu.VMEM((n_tm - 1,) + head_shape[2:], F32),
            pltpu.VMEM((n_eval - 1,) + mod_shape[1:], F32),
            e_sem, e_sem, t_sem, t_sem, t_sem, t_sem, e_sem, e_sem, e_sem, e_sem, e_sem, e_sem,
            pltpu.VMEM(head_shape, F32),
            pltpu.VMEM(mod_shape, F32),
            pltpu.VMEM(head_shape[1:], F32),
        ],
        compiler_params=params(1),
        name="reduce",
    )(
        window_start, timestep, totals, real_score, fake_score,
        hidden, modulation, head_weight, center, inv_std,
    )

    d_hidden = pl.pallas_call(
        backward_kernel,
        grid=(fd,),
        out_shape=jax.ShapeDtypeStruct(hidden.shape, BF16),
        in_specs=[
            by_frame, mod_frame, vmem, stat_frame, stat_frame,
            pl.BlockSpec((1, C * PATCH, tok), lambda f: (f, 0, 0)), stat_frame,
        ],
        out_specs=by_frame,
        scratch_shapes=[
            pltpu.VMEM((tok, width), F32),
            pltpu.VMEM((SUB, width), F32),
            pltpu.VMEM((tok, LANES), F32),
        ],
        compiler_params=params(),
        name="backward",
    )(hidden, modulation, head_weight, center, inv_std, ups, mean_b)
    return (d_hidden, head_grad, mod_grad.reshape(modulation.shape))


def solution(mesh):
    placed = (
        P("tm", "eval", None),
        P("tm", None, None),
        P(),
        P("eval", None, None, "tm"),
        P("eval", None, None, "tm"),
        P("eval"),
        P("eval"),
    )
    return jax.shard_map(
        per_device,
        mesh=mesh,
        in_specs=placed,
        out_specs=(P("tm", "eval", None), P(), P("tm", None, None)),
        check_vma=False,
    )
```
